32 devices in a mesh: view: 4 (over y, core), tile: 8 (over z, x).
Axes of the slice: x: 2, y: 2, z: 4, core: 2. Of those that a mesh axis runs over, the one named last changes fastest.
Arguments:
- objects: float32 [4, 2, 128, 1024], P('view', None, None, 'tile'), may hold values from -6 to 6
- probe: float32 [2, 128, 128], replicated, may hold values from -1.5 to 1.5
- positions: int32 [4, 64], P('view', 'tile'), may hold values from 0 to 896, as said below
- amplitudes: float32 [4, 64, 128, 128], P('view', 'tile'), may hold values from 0 to 1.0606601
- reproj_prev: float32 [4, 2, 128, 1024], P('view', None, None, 'tile'), may hold values from -6 to 6
- multipliers: float32 [4, 2, 128, 1024], P('view', None, None, 'tile'), may hold values from -4 to 4
- volume: float32 [2, 128, 1024, 1024], P(None, ('view', 'tile')), may hold values from -6 to 6
- angles: int32 [4], replicated, may hold values from 0 to 3
- penalty: int32 [2], replicated, may hold values from 1 to 5, as said below
Outputs:
- reprojections: float32 [4, 2, 128, 1024], P('view', None, None, 'tile')
- new_multipliers: float32 [4, 2, 128, 1024], P('view', None, None, 'tile')
The draws below stay inside these ranges and needn't reach their ends.
Inputs may be any that keep to these rules, and one draw needn't show every extreme that they name: `positions`: the window of a scan covers 128 columns inside the strip. The penalty is the first entry divided by the second; the first is 1 to 4, the second is 5. `angles`: angle index k is a view at k times 90 degrees.
All inputs are finite; a program needn't handle non-finite values.
Results may differ from the reference program's by a relative error of at most 0.0001.
Values sent between devices are 32-bit elements; how exact they have to be, the bound alone decides.
No kernel may reach another device: no remote copies, remote signals or barrier semaphores. Data moves between devices by JAX's collectives and lax.ppermute only.
A program may use at most 128 MiB of HBM per device.

```python
import math
import jax
import jax.numpy as jnp
from jax import lax

N = 1024
PS = 128
SLICES = 128
ITERS = 2
VIEWS = 4
SCANS = 64
COVER = 8


def draw_positions(key, part):
    starts = jax.random.randint(key, (VIEWS, SCANS), 0, N - PS + 1)
    starts = starts.at[0, 0].set(0).at[0, 1].set(N - PS)
    return starts.astype(jnp.int32)


def draw_penalty(key, part):
    upper = jax.random.randint(jax.random.fold_in(key, 11), (1,), 1, 5)
    lower = jnp.full((1,), 5, jnp.int32)
    return jnp.concatenate([upper.astype(jnp.int32), lower]).astype(jnp.int32)


def place_ends(array, rng, low, high):
    longest = array.shape.index(max(array.shape))
    spots = []
    for shift in (0, 1):
        where = [jax.random.randint(jax.random.fold_in(rng, axis), (), 0, length) for axis, length in enumerate(array.shape)]
        where[longest] = (where[longest] + shift) % array.shape[longest]
        spots.append(tuple(where))
    return array.at[spots[0]].set(low).at[spots[1]].set(high)


def levels(key, extent, split, low, top_value):
    factor_of = 1.0
    for position, blocks in split:
        heights = jax.random.uniform(jax.random.fold_in(jax.random.fold_in(key, 6), position), (blocks,), jnp.float32, low / len(split), top_value / len(split))
        factor_of = factor_of * jnp.repeat(jnp.exp(heights), extent[position] // blocks).reshape((-1,) + (1,) * (len(extent) - 1 - position))
    return factor_of


def gaussian(key, extent, scale, limit, pieces=(), kind=jnp.bfloat16):
    values = jax.random.normal(key, extent, jnp.float32) * scale
    if len(pieces) > 0:
        values = levels(key, extent, pieces, -0.22, 0.18) * values
    return jnp.clip(values, min=-limit, max=limit).astype(kind)


def setup_inputs(seed: int = 0) -> dict:
    key_list = jax.random.split(jax.random.key(seed), 10)
    return {
        "objects": gaussian(key_list[0], (VIEWS, 2, SLICES, N), 1.0, 6.0, ((0, 4), (3, 8)), jnp.float32),
        "probe": gaussian(key_list[1], (2, SLICES, PS), (2 * COVER) ** -0.5, 1.5, (), jnp.float32),
        "positions": draw_positions(jax.random.fold_in(key_list[9], 71), 0),
        "amplitudes": jnp.clip(1.0606601 * jax.random.uniform(key_list[3], (VIEWS, SCANS, SLICES, PS), jnp.float32) ** levels(key_list[3], (VIEWS, SCANS, SLICES, PS), ((0, 4), (1, 8)), -0.2, 0.2), 0.0, 1.0606601),
        "reproj_prev": gaussian(key_list[4], (VIEWS, 2, SLICES, N), 1.0, 6.0, ((0, 4), (3, 8)), jnp.float32),
        "multipliers": gaussian(key_list[5], (VIEWS, 2, SLICES, N), 0.5, 4.0, ((0, 4), (3, 8)), jnp.float32),
        "volume": gaussian(key_list[6], (2, SLICES, N, N), 1.0, 6.0, ((1, 32),), jnp.float32),
        "angles": place_ends(jax.random.randint(key_list[7], (VIEWS,), 0, 4), jax.random.fold_in(key_list[7], 1), 0, 3).astype(jnp.int32),
        "penalty": draw_penalty(jax.random.fold_in(key_list[9], 71), 0),
    }


HIGHEST = lax.Precision.HIGHEST

def dft_tables(length):
    indices = jnp.arange(length, dtype=jnp.int32)
    phase = (indices[:, None] * indices[None, :] % length).astype(jnp.float32) * (2.0 * math.pi / length)
    factor = 1.0 / math.sqrt(length)
    return (jnp.cos(phase) * factor, -jnp.sin(phase) * factor)

def left_apply(cosine, sine, sign, real_part, imag_part):
    first = jnp.einsum('rk,nkc->nrc', cosine, real_part, precision=HIGHEST)
    second = jnp.einsum('rk,nkc->nrc', sine, imag_part, precision=HIGHEST)
    third = jnp.einsum('rk,nkc->nrc', cosine, imag_part, precision=HIGHEST)
    fourth = jnp.einsum('rk,nkc->nrc', sine, real_part, precision=HIGHEST)
    return (first - sign * second, third + sign * fourth)

def right_apply(cosine, sine, sign, real_part, imag_part):
    first = jnp.einsum('nrk,kc->nrc', real_part, cosine, precision=HIGHEST)
    second = jnp.einsum('nrk,kc->nrc', imag_part, sine, precision=HIGHEST)
    third = jnp.einsum('nrk,kc->nrc', imag_part, cosine, precision=HIGHEST)
    fourth = jnp.einsum('nrk,kc->nrc', real_part, sine, precision=HIGHEST)
    return (first - sign * second, third + sign * fourth)

def window_columns(starts, width):
    return (starts[:, None] + jnp.arange(width, dtype=jnp.int32)[None, :]).reshape(-1)

def strip_gradient(strip, starts, measured, probe, floor):
    rows = strip.shape[1]
    width = probe.shape[2]
    total = strip.shape[2]
    windows = jax.vmap(lambda start: lax.dynamic_slice_in_dim(strip, start, width, axis=2))(starts)
    window_re = windows[:, 0]
    window_im = windows[:, 1]
    probe_re = probe[0]
    probe_im = probe[1]
    exit_re = probe_re * window_re - probe_im * window_im
    exit_im = probe_re * window_im + probe_im * window_re
    row_cos, row_sin = dft_tables(rows)
    col_cos, col_sin = dft_tables(width)
    mid_re, mid_im = left_apply(row_cos, row_sin, 1.0, exit_re, exit_im)
    far_re, far_im = right_apply(col_cos, col_sin, 1.0, mid_re, mid_im)
    modulus = jnp.sqrt(far_re * far_re + far_im * far_im)
    keep = 1.0 - measured / jnp.maximum(modulus, floor)
    back_re, back_im = left_apply(row_cos, row_sin, -1.0, far_re * keep, far_im * keep)
    back_re, back_im = right_apply(col_cos, col_sin, -1.0, back_re, back_im)
    grad_re = probe_re * back_re + probe_im * back_im
    grad_im = probe_re * back_im - probe_im * back_re
    columns = window_columns(starts, width)
    values = jnp.stack([grad_re, grad_im], axis=0).transpose(0, 2, 1, 3).reshape(2, rows, -1)
    return jnp.zeros((2, rows, total), jnp.float32).at[:, :, columns].add(values)

def illumination(starts, probe, total):
    rows = probe.shape[1]
    width = probe.shape[2]
    power = probe[0] * probe[0] + probe[1] * probe[1]
    values = jnp.broadcast_to(power[:, None, :], (rows, starts.shape[0], width)).reshape(rows, -1)
    return jnp.zeros((rows, total), jnp.float32).at[:, window_columns(starts, width)].add(values)

def project(column_sum, row_sum, angles):
    length = column_sum.shape[-1]
    angle_grid = angles[:, None]
    along = column_sum[..., None, :]
    across = row_sum[..., None, :]
    result = jnp.where(angle_grid == 0, along, jnp.where(angle_grid == 1, across, jnp.where(angle_grid == 2, jnp.flip(along, -1), jnp.flip(across, -1))))
    return result * (1.0 / math.sqrt(length))

def backproject(lines, angles):
    length = lines.shape[-1]
    angle_grid = angles[:, None]
    zero = jnp.zeros_like(lines)
    column_term = lax.optimization_barrier(jnp.sum(jnp.where(angle_grid == 0, lines, zero), -2)) + jnp.flip(lax.optimization_barrier(jnp.sum(jnp.where(angle_grid == 2, lines, zero), -2)), -1)
    row_term = lax.optimization_barrier(jnp.sum(jnp.where(angle_grid == 1, lines, zero), -2)) + jnp.flip(lax.optimization_barrier(jnp.sum(jnp.where(angle_grid == 3, lines, zero), -2)), -1)
    return (column_term[..., None, :] + row_term[..., :, None]) * (1.0 / math.sqrt(length))

def reference(objects, probe, positions, amplitudes, reproj_prev, multipliers, volume, angles, penalty):
    penalty_value = penalty[0].astype(jnp.float32) / penalty[1].astype(jnp.float32)
    floor = 0.25 / math.sqrt(COVER)

    def one_view(inputs):
        strip, starts, measured, previous, lagrange = inputs
        power = illumination(starts, probe, strip.shape[2])
        for sweep in range(ITERS):
            grad = strip_gradient(strip, starts, measured, probe, floor)
            strip = strip - (grad + penalty_value * (strip - previous) + lagrange) / (power + penalty_value)
        return strip
    psi = lax.map(one_view, (objects, positions, amplitudes, reproj_prev, multipliers))
    views = objects.shape[0]

    def one_slice(index):
        slab = lax.dynamic_index_in_dim(volume, index, 1, keepdims=False)
        lines = jnp.transpose(lax.dynamic_index_in_dim(psi, index, 2, keepdims=False), (1, 0, 2))
        lagrange = jnp.transpose(lax.dynamic_index_in_dim(multipliers, index, 2, keepdims=False), (1, 0, 2))
        projected = project(slab.sum(1), slab.sum(2), angles)
        misfit = projected - lines - lagrange / penalty_value
        updated = slab - backproject(misfit, angles) / views
        fresh = project(updated.sum(1), updated.sum(2), angles)
        return (fresh, lagrange + penalty_value * (lines - fresh))
    fresh, lagrange = lax.map(one_slice, jnp.arange(SLICES, dtype=jnp.int32))
    return (jnp.transpose(fresh, (2, 1, 0, 3)), jnp.transpose(lagrange, (2, 1, 0, 3)))
```

```python
import functools
import math

import jax
import jax.numpy as jnp
import numpy as np
from jax import lax
from jax.experimental import pallas as pl
from jax.experimental.pallas import tpu as pltpu
from jax.sharding import PartitionSpec as P

ITERS = 2
AXES = ("view", "tile")
VMEM = pl.BlockSpec(memory_space=pltpu.VMEM)
SMEM = pl.BlockSpec(memory_space=pltpu.SMEM)
LIMIT = pltpu.CompilerParams(vmem_limit_bytes=48 * 2**20)
HIGHEST = lax.Precision.HIGHEST


class Routes:
    def __init__(self, views, tiles):
        self.views, self.tiles, self.half = views, tiles, tiles // 2
        self.hubs = (tiles // 4, tiles - 1 - tiles // 4)

    def at(self, view, tile):
        return view * self.tiles + tile

    def to_hub(self, part, swap):
        return [
            (
                self.at(2 * k + b, j * self.half + (part ^ b if swap else part)),
                self.at(2 * k + j, self.hubs[b]),
            )
            for k in range(self.views // 2)
            for b in range(2)
            for j in range(2)
        ]

    def from_hub(self, part):
        return [(target, source) for source, target in self.to_hub(part, False)]

    def cores(self):
        return [
            (self.at(v, t), self.at(v ^ 1, t)) for v in range(self.views) for t in range(self.tiles)
        ]


def send(value, pairs):
    return lax.ppermute(value, AXES, pairs)


def dft(length):
    indices = np.arange(length)
    phase = (indices[:, None] * indices[None, :] % length) * (2.0 * math.pi / length)
    return np.cos(phase) / math.sqrt(length), -np.sin(phase) / math.sqrt(length)


def halves(matrix):
    high = matrix.astype(jnp.bfloat16)
    return high, (matrix - high.astype(np.float64)).astype(jnp.bfloat16)


def tables(rows, width):
    result = []
    cosine, sine = dft(rows)
    for sign in (1.0, -1.0):
        high, low = halves(np.block([[cosine, -sign * sine], [sign * sine, cosine]]))
        result.append(np.concatenate([high, low, high], 1))
    cosine, sine = dft(width)
    for sign in (1.0, -1.0):
        high, low = halves(np.block([[cosine, sign * sine], [-sign * sine, cosine]]))
        result.append(np.concatenate([high, low, high], 0))
    return [jnp.asarray(table) for table in result]


def split(value):
    high = value.astype(jnp.bfloat16)
    return high, (value - high.astype(jnp.float32)).astype(jnp.bfloat16)


def left(table, value):
    high, low = split(value)
    return jnp.dot(
        table, jnp.concatenate([high, high, low], 0), preferred_element_type=jnp.float32
    )


def right(value, table):
    high, low = split(value)
    return jnp.dot(
        jnp.concatenate([high, high, low], 1), table, preferred_element_type=jnp.float32
    )


def place(meta, index, chunks, width):
    start = meta[index]
    chunk = start // width
    offset = meta[meta.shape[0] - 2]
    here = lax.rem(chunk + offset, chunks)
    after = lax.rem(jnp.minimum(chunk + 1, chunks - 1) + offset, chunks)
    return here, after, start - chunk * width


def gather_chunks(refs, strip):
    at = 0
    for ref in refs:
        if len(ref.shape) == 3:
            strip[at : at + ref.shape[0]] = ref[...]
            at += ref.shape[0]
        else:
            strip[at] = ref[: strip.shape[1]]
            at += 1


def gradient_kernel(floor, part_list, n_strip, n_parts, first, meta, *refs):
    pieces, refs = refs[:n_strip], refs[n_strip:]
    measured, refs = refs[:n_parts], refs[n_parts:]
    probe, forward_left, back_left, forward_right, back_right = refs[:5]
    refs = refs[5:]
    if not first:
        before, refs = refs[0], refs[1:]
    grad, strip = refs
    chunks = strip.shape[0]
    _, rows, width = probe.shape
    gather_chunks(pieces, strip)
    if first:
        grad[...] = jnp.zeros_like(grad)
    else:
        grad[...] = before[...]
    lane = lax.broadcasted_iota(jnp.int32, (rows, width), 1)
    probe_re = probe[0]
    probe_im = probe[1]
    swapped = meta[meta.shape[0] - 1]
    def work(part, amplitude):
        batch = amplitude.shape[0]
        row = part + swapped * (1 - 2 * lax.rem(part, 2))
        columns = []
        spots = []
        for j in range(batch):
            here, after, shift = place(meta, row * batch + j, chunks, width)
            spots.append((here, after, shift))
            back = lax.rem(width - shift, width)
            keep = lane < width - shift
            re, im = [
                jnp.where(
                    keep,
                    pltpu.roll(strip[here, k * rows : (k + 1) * rows], back, 1),
                    pltpu.roll(strip[after, k * rows : (k + 1) * rows], back, 1),
                )
                for k in range(2)
            ]
            columns.append(
                jnp.concatenate(
                    [probe_re * re - probe_im * im, probe_re * im + probe_im * re], 0
                )
            )
        mid = left(forward_left[...], jnp.concatenate(columns, 1))
        mid = jnp.concatenate(
            [
                jnp.concatenate(
                    [
                        mid[:rows, j * width : (j + 1) * width],
                        mid[rows:, j * width : (j + 1) * width],
                    ],
                    1,
                )
                for j in range(batch)
            ],
            0,
        )
        far = right(mid, forward_right[...])
        far_re = far[:, :width]
        far_im = far[:, width:]
        level = amplitude[...].reshape(batch * rows, width)
        keep = 1.0 - level * jnp.minimum(
            lax.rsqrt(far_re * far_re + far_im * far_im), 1.0 / floor
        )
        mid = right(jnp.concatenate([far_re * keep, far_im * keep], 1), back_right[...])
        mid = jnp.concatenate(
            [
                jnp.concatenate(
                    [
                        mid[j * rows : (j + 1) * rows, :width],
                        mid[j * rows : (j + 1) * rows, width:],
                    ],
                    0,
                )
                for j in range(batch)
            ],
            1,
        )
        back = left(back_left[...], mid)
        for j in range(batch):
            here, after, shift = spots[j]
            back_re = back[:rows, j * width : (j + 1) * width]
            back_im = back[rows:, j * width : (j + 1) * width]
            inside = lane >= shift
            for k, value in enumerate(
                (
                    probe_re * back_re + probe_im * back_im,
                    probe_re * back_im - probe_im * back_re,
                )
            ):
                value = pltpu.roll(value, shift, 1)
                band = slice(k * rows, (k + 1) * rows)
                grad[here, band] += jnp.where(inside, value, 0.0)
                grad[after, band] += jnp.where(inside, 0.0, value)

    if len(part_list) == n_parts:
        for part, amplitude in zip(part_list, measured):
            work(part, amplitude)
    else:

        def step(index, carry):
            work(index, measured[0].at[index])
            return carry

        lax.fori_loop(0, measured[0].shape[0], step, 0)


def gradient(meta, pieces, measured, part_list, probe, dft_tables, floor, chunks, before):
    _, rows, width = probe.shape
    shape = (chunks, 2 * rows, width)
    carried = [] if before is None else [before]
    count = 1 + len(pieces) + len(measured) + 1 + len(dft_tables)
    return pl.pallas_call(
        functools.partial(
            gradient_kernel,
            floor,
            tuple(part_list),
            len(pieces),
            len(measured),
            before is None,
        ),
        out_shape=jax.ShapeDtypeStruct(shape, jnp.float32),
        in_specs=[SMEM] + [VMEM] * (count - 1 + len(carried)),
        out_specs=VMEM,
        scratch_shapes=[pltpu.VMEM(shape, jnp.float32)],
        input_output_aliases={} if before is None else {count: 0},
        compiler_params=LIMIT,
    )(meta, *pieces, *measured, probe, *dft_tables, *carried)


def illumination_kernel(meta, probe, power):
    chunks = power.shape[0]
    _, rows, width = probe.shape
    power[...] = jnp.zeros_like(power)
    lane = lax.broadcasted_iota(jnp.int32, (rows, width), 1)
    value = probe[0] * probe[0] + probe[1] * probe[1]

    def step(index, carry):
        here, after, shift = place(meta, index, chunks, width)
        rolled = pltpu.roll(value, shift, 1)
        power[here] += jnp.where(lane >= shift, rolled, 0.0)
        power[after] += jnp.where(lane >= shift, 0.0, rolled)
        return carry

    lax.fori_loop(0, meta.shape[0] - 2, step, 0)


def illumination(meta, probe, chunks):
    _, rows, width = probe.shape
    return pl.pallas_call(
        illumination_kernel,
        out_shape=jax.ShapeDtypeStruct((chunks, rows, width), jnp.float32),
        in_specs=[SMEM, VMEM],
        out_specs=VMEM,
        compiler_params=LIMIT,
    )(meta, probe)


def update_kernel(n_strip, n_pull, rho, *refs):
    pieces, refs = refs[:n_strip], refs[n_strip:]
    pulls, refs = refs[:n_pull], refs[n_pull:]
    grad, grad_other, power, power_other, out = refs
    count = out.shape[0]
    rows = power.shape[1]
    ratio = rho[0]
    for chunk in range(count):
        inverse = 1.0 / (power[chunk] + power_other[chunk] + ratio)
        for k in range(2):
            band = slice(k * rows, (k + 1) * rows)
            old = pieces[0][chunk, band] if n_strip == 1 else pieces[chunk][band]
            pull = pulls[0][chunk, band] if n_pull == 1 else pulls[chunk][band]
            step = grad[chunk, band] + grad_other[chunk, band] + ratio * old - pull
            out[chunk, band] = old - step * inverse


def update(rho, pieces, pulls, grad, grad_other, power, power_other):
    own = power_other.shape[0]
    return pl.pallas_call(
        functools.partial(update_kernel, len(pieces), len(pulls)),
        out_shape=jax.ShapeDtypeStruct((own,) + grad.shape[1:], jnp.float32),
        in_specs=[SMEM] + [VMEM] * (len(pieces) + len(pulls) + 4),
        out_specs=VMEM,
        compiler_params=LIMIT,
    )(rho, *pieces, *pulls, grad, grad_other, power, power_other)


def sums_kernel(block, column, row, partial):
    index = pl.program_id(0)
    step = pl.program_id(1)
    _, rows, length = block.shape
    value = block[0]
    down = value.reshape(rows // 8, 8, length).sum(0)

    @pl.when(step == 0)
    def _():
        partial[...] = down

    @pl.when(step > 0)
    def _():
        partial[...] += down

    @pl.when(step == pl.num_programs(1) - 1)
    def _():
        column[pl.ds(index, 1), :] = partial[...].sum(0, keepdims=True)

    across = value.reshape(rows, length)
    lanes = 128
    folded = across[:, :lanes]
    for k in range(1, length // lanes):
        folded = folded + across[:, k * lanes : (k + 1) * lanes]
    line = lax.dot_general(
        jnp.ones((8, lanes), jnp.float32),
        folded,
        (((1,), (1,)), ((), ())),
        precision=HIGHEST,
        preferred_element_type=jnp.float32,
    )
    row[pl.ds(index, 1), pl.ds(pl.multiple_of(step * rows, rows), rows)] = line[:1]


def volume_sums(volume):
    planes, length, _ = volume.shape
    rows = length // 2
    out = jax.ShapeDtypeStruct((planes, length), jnp.float32)
    return pl.pallas_call(
        sums_kernel,
        grid=(planes, length // rows),
        out_shape=(out, out),
        in_specs=[pl.BlockSpec((1, rows, length), lambda i, k: (i, k, 0))],
        out_specs=(
            pl.BlockSpec((planes, length), lambda i, k: (0, 0)),
            pl.BlockSpec((planes, length), lambda i, k: (0, 0)),
        ),
        scratch_shapes=[pltpu.VMEM((8, length), jnp.float32)],
        compiler_params=LIMIT,
    )(volume)


def pack_kernel(n_parts, rho, *refs):
    parts, (lagrange, psi, packed) = refs[:n_parts], refs[n_parts:]
    owners, planes, _ = packed.shape
    owned = planes // 2
    for k in range(2):
        value = parts[0][k]
        for part in parts[1:]:
            value = value + part[k]
        psi[k] = value
        value = value + lagrange[k] / rho[0]
        packed[:, k * owned : (k + 1) * owned, :] = value.reshape(owners, owned, value.shape[1])


def slice_kernel(views, angles, lines, column, row, out):
    total, planes, width = lines.shape
    tiles = total // views
    length = column.shape[1]
    scale = 1.0 / math.sqrt(length)
    rows_of = lax.broadcasted_iota(jnp.int32, (width, width), 0)
    columns_of = lax.broadcasted_iota(jnp.int32, (width, width), 1)
    mirror = jnp.where(rows_of + columns_of == width - 1, 1.0, 0.0).astype(jnp.float32)

    def flip(values):
        stacked = jnp.dot(
            jnp.concatenate(values, 0),
            mirror,
            precision=HIGHEST,
            preferred_element_type=jnp.float32,
        )
        return [stacked[k * planes : (k + 1) * planes] for k in range(len(values))]

    base = []
    plain = []
    turned = []
    count = []
    for parity, source in ((0, column), (1, row)):
        for t in range(tiles):
            base.append(source[:, t * width : (t + 1) * width] * scale)
            plain.append(
                sum(
                    jnp.where(angles[u] == parity, lines[u * tiles + t], 0.0)
                    for u in range(views)
                )
            )
            turned.append(
                sum(
                    jnp.where(angles[u] == parity + 2, lines[u * tiles + tiles - 1 - t], 0.0)
                    for u in range(views)
                )
            )
        count.append(
            sum(
                jnp.where((angles[u] == parity) | (angles[u] == parity + 2), 1.0, 0.0)
                for u in range(views)
            )
        )
    turned = flip(turned)
    misfit = [
        base[parity * tiles + t] * count[parity]
        - plain[parity * tiles + t]
        - turned[parity * tiles + t]
        for parity in range(2)
        for t in range(tiles)
    ]
    total_of = [
        jnp.sum(
            functools.reduce(jnp.add, misfit[parity * tiles : (parity + 1) * tiles]),
            1,
            keepdims=True,
        )
        * (1.0 / length)
        for parity in range(2)
    ]
    fresh = [
        base[parity * tiles + t]
        - (misfit[parity * tiles + t] + total_of[1 - parity]) * (1.0 / views)
        for parity in range(2)
        for t in range(tiles)
    ]
    reversed_fresh = flip(fresh)
    for u in range(views):
        for t in range(tiles):
            out[u * tiles + t] = jnp.where(
                angles[u] == 0,
                fresh[t],
                jnp.where(
                    angles[u] == 1,
                    fresh[tiles + t],
                    jnp.where(
                        angles[u] == 2,
                        reversed_fresh[tiles - 1 - t],
                        reversed_fresh[2 * tiles - 1 - t],
                    ),
                ),
            )


def final_kernel(rho, packed, psi, lagrange, fresh, renewed):
    owners, planes, width = packed.shape
    owned = planes // 2
    for k in range(2):
        value = packed[:, k * owned : (k + 1) * owned, :].reshape(owners * owned, width)
        fresh[k] = value
        renewed[k] = lagrange[k] + rho[0] * (psi[k] - value)


def shards(
    objects, probe, positions, amplitudes, reproj_prev, multipliers, volume, angles, penalty
):
    tiles = lax.axis_size("tile")
    views = lax.axis_size("view")
    routes = Routes(views, tiles)
    half = routes.half
    _, _, rows, tile_width = objects.shape
    width = probe.shape[2]
    total = tile_width * tiles
    chunks = total // width
    scans = positions.shape[1]
    owned = volume.shape[1]
    floor = 0.25 / math.sqrt(scans * tiles * width // total)
    rho = penalty[0].astype(jnp.float32) / penalty[1].astype(jnp.float32)
    rho_array = rho[None]
    lagrange = multipliers[0]
    measured = amplitudes[0]
    core = lax.rem(lax.axis_index("view"), 2)
    swapped = (lax.axis_index("tile") == routes.hubs[1]).astype(jnp.int32)
    dft_tables = tables(rows, width)

    def as_chunks(parts):
        if tile_width == width:
            return parts
        joined = jnp.stack([part[: 2 * rows] for part in parts], 0)
        joined = joined.reshape(chunks // 2, width // tile_width, 2 * rows, tile_width)
        return [joined.transpose(0, 2, 1, 3).reshape(chunks // 2, 2 * rows, width)]

    def as_tiles(own):
        if tile_width == width:
            return [own[part].reshape(2, rows, width) for part in range(half)]
        parts = own.reshape(chunks // 2, 2 * rows, width // tile_width, tile_width)
        parts = parts.transpose(0, 2, 1, 3).reshape(half, 2, rows, tile_width)
        return [parts[part] for part in range(half)]

    pad = -scans % tile_width
    starts = jnp.pad(positions.astype(jnp.float32), ((0, 0), (0, pad))).reshape(-1, tile_width)
    starts = jnp.pad(starts, ((0, -starts.shape[0] % 8), (0, 0)))
    message = jnp.concatenate([objects.reshape(2 * rows, tile_width), starts], 0)
    arrived = [send(message, routes.to_hub(part, False)) for part in range(half)]
    levels = [send(measured, routes.to_hub(part, True)) for part in range(half)]
    pull = (rho * reproj_prev - multipliers).reshape(2 * rows, tile_width)
    pulls = as_chunks([send(pull, routes.to_hub(part, False)) for part in range(half)])
    column, row = volume_sums(volume.reshape(2 * owned, total, total))

    meta = jnp.concatenate(
        [part[2 * rows :].reshape(-1)[:scans].astype(jnp.int32) for part in arrived]
        + [(core * (chunks // 2))[None], swapped[None]]
    )
    own = as_chunks(arrived)
    other = [send(part, routes.cores()) for part in own]
    power = illumination(meta, probe, chunks)
    power_other = send(power[chunks // 2 :], routes.cores())

    grad = None
    if half > 4:
        levels = [jnp.stack(levels, 0)]
        grad = gradient(
            meta, own + other, levels, range(half), probe, dft_tables, floor, chunks, None
        )
    else:
        for part in range(half):
            grad = gradient(
                meta, own + other, [levels[part]], [part], probe, dft_tables, floor, chunks, grad
            )
    for sweep in range(ITERS):
        grad_other = send(grad[chunks // 2 :], routes.cores())
        mine = update(rho_array, own, pulls, grad, grad_other, power, power_other)
        if sweep + 1 < ITERS:
            own = [mine]
            other = [send(mine, routes.cores())]
            grad = gradient(
                meta, own + other, levels, range(half), probe, dft_tables, floor, chunks, None
            )

    parts = [send(part, routes.from_hub(index)) for index, part in enumerate(as_tiles(mine))]
    strip = jax.ShapeDtypeStruct((2, rows, tile_width), jnp.float32)
    owners = views * tiles
    exchanged = jax.ShapeDtypeStruct((owners, 2 * owned, tile_width), jnp.float32)
    psi, packed = pl.pallas_call(
        functools.partial(pack_kernel, len(parts)),
        out_shape=(strip, exchanged),
        in_specs=[SMEM] + [VMEM] * (len(parts) + 1),
        out_specs=(VMEM, VMEM),
        compiler_params=LIMIT,
    )(rho_array, *parts, lagrange)
    lines = lax.all_to_all(packed, AXES, split_axis=0, concat_axis=0, tiled=True)
    fresh = pl.pallas_call(
        functools.partial(slice_kernel, views),
        out_shape=exchanged,
        in_specs=[SMEM] + [VMEM] * 3,
        out_specs=VMEM,
        compiler_params=LIMIT,
    )(angles, lines, column, row)
    fresh = lax.all_to_all(fresh, AXES, split_axis=0, concat_axis=0, tiled=True)
    fresh_strip, renewed = pl.pallas_call(
        final_kernel,
        out_shape=(strip, strip),
        in_specs=[SMEM] + [VMEM] * 3,
        out_specs=(VMEM, VMEM),
        compiler_params=LIMIT,
    )(rho_array, fresh, psi, lagrange)
    return (fresh_strip[None], renewed[None])


def solution(mesh):
    return jax.shard_map(
        shards,
        mesh=mesh,
        in_specs=(
            P("view", None, None, "tile"),
            P(),
            P("view", "tile"),
            P("view", "tile", None, None),
            P("view", None, None, "tile"),
            P("view", None, None, "tile"),
            P(None, ("view", "tile"), None, None),
            P(),
            P(),
        ),
        out_specs=(P("view", None, None, "tile"), P("view", None, None, "tile")),
        check_vma=False,
    )
```

```python
import functools
import math

import jax
import jax.numpy as jnp
import numpy as np
from jax import lax
from jax.experimental import pallas as pl
from jax.experimental.pallas import tpu as pltpu
from jax.sharding import PartitionSpec as P

ITERS = 2
AXES = ("view", "tile")
VMEM = pl.BlockSpec(memory_space=pltpu.VMEM)
SMEM = pl.BlockSpec(memory_space=pltpu.SMEM)
HBM = pl.BlockSpec(memory_space=pltpu.HBM)
COST = pl.CostEstimate(flops=0, bytes_accessed=0, transcendentals=0)
LIMIT = pltpu.CompilerParams(vmem_limit_bytes=16 * 2**20)
HIGHEST = lax.Precision.HIGHEST


class Routes:
    def __init__(self, views, tiles):
        self.views, self.tiles, self.half = views, tiles, tiles // 2
        self.hubs = (tiles // 4, tiles - 1 - tiles // 4)

    def at(self, view, tile):
        return view * self.tiles + tile

    def to_hub(self, part, swap):
        return [
            (
                self.at(2 * k + b, j * self.half + (self.turn(part, b) if swap else part)),
                self.at(2 * k + j, self.hubs[b]),
            )
            for k in range(self.views // 2)
            for b in range(2)
            for j in range(2)
        ]

    def from_hub(self, part):
        return [(target, source) for source, target in self.to_hub(part, False)]

    def turn(self, part, b):
        return self.half - 1 - part if b else part

    def relays(self):
        return [
            (self.at(v, tile), self.at(v, tile ^ 1))
            for v in range(self.views)
            for tile in ((self.tiles - 2 if v % 2 else 1),)
        ]

    def relayed(self, part):
        hops = dict(self.relays())
        return [(hops.get(source, source), target) for source, target in self.to_hub(part, True)]

    def cores(self):
        return [
            (self.at(v, t), self.at(v ^ 1, t)) for v in range(self.views) for t in self.hubs
        ]


def send(value, pairs):
    return lax.ppermute(value, AXES, pairs)


def dft(length):
    indices = np.arange(length)
    phase = (indices[:, None] * indices[None, :] % length) * (2.0 * math.pi / length)
    return np.cos(phase) / math.sqrt(length), -np.sin(phase) / math.sqrt(length)


def halves(matrix):
    high = matrix.astype(jnp.bfloat16)
    return high, (matrix - high.astype(np.float64)).astype(jnp.bfloat16)


def tables(rows, width):
    result = []
    for length in (rows, width):
        cosine, sine = dft(length)
        for sign in (1.0, -1.0):
            result.append(halves(np.block([[cosine, -sign * sine], [sign * sine, cosine]])))
    return jnp.asarray(np.array(result[:2] if rows == width else result))


def split(value):
    high = value.astype(jnp.bfloat16)
    return high, (value - high.astype(jnp.float32)).astype(jnp.bfloat16)


def left(table, value):
    high, low = split(value)
    first, second = table
    return jnp.dot(
        jnp.concatenate([first, second, first], 1),
        jnp.concatenate([high, high, low], 0),
        preferred_element_type=jnp.float32,
    )


def right(value, table):
    high, low = split(value)
    first, second = table
    return jnp.dot(
        jnp.concatenate([high, high, low], 1),
        jnp.concatenate([first, second, first], 0),
        preferred_element_type=jnp.float32,
    )


def place(meta, index, chunks, width):
    start = meta[index]
    chunk = start // width
    offset = meta[meta.shape[0] - 2]
    here = lax.rem(chunk + offset, chunks)
    after = lax.rem(jnp.minimum(chunk + 1, chunks - 1) + offset, chunks)
    return here, after, start - chunk * width


def sum_plane(plane, folded, lanes):
    rows, length = plane.shape

    def step(index, down):
        base = pl.multiple_of(index * lanes, lanes)
        for at in range(0, lanes, 8):
            value = plane[pl.ds(base + at, 8)]
            down = down + value
            parts = [value[:, k : k + lanes] for k in range(0, length, lanes)]
            while len(parts) > 1:
                parts = [first + second for first, second in zip(parts[::2], parts[1::2])]
            folded[pl.ds(base + at, 8)] = parts[0]
        return down

    down = lax.fori_loop(0, rows // lanes, step, jnp.zeros((8, length), jnp.float32))
    lines = [folded[at : at + lanes].T.sum(0, keepdims=True) for at in range(0, rows, lanes)]
    return down, jnp.concatenate(lines, 1)


def gradient_kernel(floor, part_list, n_parts, first, scans, meta, own, other, *refs):
    measured, refs = refs[:n_parts], refs[n_parts:]
    probe, table, refs = refs[0], refs[1], refs[2:]
    if not first:
        before, refs = refs[0], refs[1:]
    grad, strip = refs
    chunks = strip.shape[0]
    _, rows, width = probe.shape
    strip[: chunks // 2] = own[:, : 2 * rows]
    strip[chunks // 2 :] = other[:, : 2 * rows]
    if first:
        grad[...] = jnp.zeros_like(grad)
    else:
        grad[...] = before[...]
    lane = lax.broadcasted_iota(jnp.int32, (rows, width), 1)
    probe_re = probe[0]
    probe_im = probe[1]
    swapped = meta[meta.shape[0] - 1]

    def get(index):
        return table[index, 0], table[index, 1]

    across = table.shape[0] - 2

    def work(part, amplitude, batch):
        row = part + swapped * (meta.shape[0] // scans - 1 - 2 * part)
        columns = []
        spots = []
        for j in range(batch):
            here, after, shift = place(meta, row * batch + j, chunks, width)
            spots.append((here, after, shift))
            back = lax.rem(width - shift, width)
            keep = lane < width - shift
            re, im = [
                jnp.where(
                    keep,
                    pltpu.roll(strip[here, k * rows : (k + 1) * rows], back, 1),
                    pltpu.roll(strip[after, k * rows : (k + 1) * rows], back, 1),
                )
                for k in range(2)
            ]
            columns.append(
                jnp.concatenate(
                    [probe_re * re - probe_im * im, probe_re * im + probe_im * re], 0
                )
            )
        mid = left(get(0), jnp.concatenate(columns, 1))
        mid = jnp.concatenate(
            [
                jnp.concatenate(
                    [
                        mid[:rows, j * width : (j + 1) * width],
                        mid[rows:, j * width : (j + 1) * width],
                    ],
                    1,
                )
                for j in range(batch)
            ],
            0,
        )
        far = right(mid, get(across + 1))
        far_re = far[:, :width]
        far_im = far[:, width:]
        level = amplitude[:batch].reshape(batch * rows, width)
        keep = 1.0 - level * jnp.minimum(
            lax.rsqrt(far_re * far_re + far_im * far_im), 1.0 / floor
        )
        mid = right(jnp.concatenate([far_re * keep, far_im * keep], 1), get(across))
        mid = jnp.concatenate(
            [
                jnp.concatenate(
                    [
                        mid[j * rows : (j + 1) * rows, :width],
                        mid[j * rows : (j + 1) * rows, width:],
                    ],
                    0,
                )
                for j in range(batch)
            ],
            1,
        )
        back = left(get(1), mid)
        for j in range(batch):
            here, after, shift = spots[j]
            back_re = back[:rows, j * width : (j + 1) * width]
            back_im = back[rows:, j * width : (j + 1) * width]
            inside = lane >= shift
            for k, value in enumerate(
                (
                    probe_re * back_re + probe_im * back_im,
                    probe_re * back_im - probe_im * back_re,
                )
            ):
                value = pltpu.roll(value, shift, 1)
                band = slice(k * rows, (k + 1) * rows)
                grad[here, band] += jnp.where(inside, value, 0.0)
                grad[after, band] += jnp.where(inside, 0.0, value)

    if len(part_list) == n_parts:
        for part, amplitude in zip(part_list, measured):
            work(part, amplitude, scans)
    else:

        def step(index, carry):
            work(index, measured[0].at[index], scans)
            return carry

        lax.fori_loop(0, measured[0].shape[0], step, 0)


def gradient(meta, own, other, measured, part_list, scans, probe, dft_tables, floor, before):
    _, rows, width = probe.shape
    chunks = own.shape[0] * 2
    shape = (chunks, 2 * rows, width)
    carried = [] if before is None else [before]
    count = 3 + len(measured) + 2
    return pl.pallas_call(
        functools.partial(
            gradient_kernel, floor, tuple(part_list), len(measured), before is None, scans
        ),
        out_shape=jax.ShapeDtypeStruct(shape, jnp.float32),
        in_specs=[SMEM] + [VMEM] * (count - 1 + len(carried)),
        out_specs=VMEM,
        scratch_shapes=[pltpu.VMEM(shape, jnp.float32)],
        input_output_aliases={} if before is None else {count: 0},
        cost_estimate=COST,
        compiler_params=pltpu.CompilerParams(vmem_limit_bytes=24 * 2**20),
    )(meta, own, other, *measured, probe, dft_tables, *carried)


def illumination_kernel(meta, probe, power):
    chunks = power.shape[0]
    _, rows, width = probe.shape
    power[...] = jnp.zeros_like(power)
    lane = lax.broadcasted_iota(jnp.int32, (rows, width), 1)
    value = probe[0] * probe[0] + probe[1] * probe[1]

    group = 8

    def step(index, carry):
        for j in range(group):
            here, after, shift = place(meta, index * group + j, chunks, width)
            rolled = pltpu.roll(value, shift, 1)
            power[here] += jnp.where(lane >= shift, rolled, 0.0)
            power[after] += jnp.where(lane >= shift, 0.0, rolled)
        return carry

    lax.fori_loop(0, (meta.shape[0] - 2) // group, step, 0)


def illumination(meta, probe, chunks):
    _, rows, width = probe.shape
    return pl.pallas_call(
        illumination_kernel,
        out_shape=jax.ShapeDtypeStruct((chunks, rows, width), jnp.float32),
        in_specs=[SMEM, VMEM],
        out_specs=VMEM,
        cost_estimate=COST,
        compiler_params=LIMIT,
    )(meta, probe)


def update_kernel(n_pull, penalty, meta, own, *refs):
    pulls, refs = refs[:n_pull], refs[n_pull:]
    grad, grad_other, power, power_other, out = refs
    count = out.shape[0]
    rows = power.shape[1]
    ratio = ratio_of(penalty)
    swapped = meta[meta.shape[0] - 1] == 1
    for chunk in range(count):
        inverse = 1.0 / (power[chunk] + power_other[chunk] + ratio)
        for k in range(2):
            band = slice(k * rows, (k + 1) * rows)
            old = own[chunk, band]
            if n_pull == 1:
                pull = pulls[0][chunk, band]
            else:
                last = pulls[0].shape[0] - 2 + k
                pull = jnp.where(swapped, pulls[count - 1 - chunk][last], pulls[chunk][last])
            step = grad[chunk, band] + grad_other[chunk, band] + ratio * old - pull
            out[chunk, band] = old - step * inverse


def update(penalty, meta, own, pulls, grad, grad_other, power, power_other):
    count = power_other.shape[0]
    return pl.pallas_call(
        functools.partial(update_kernel, len(pulls)),
        out_shape=jax.ShapeDtypeStruct((count,) + grad.shape[1:], jnp.float32),
        in_specs=[SMEM, SMEM] + [VMEM] * (len(pulls) + 5),
        out_specs=VMEM,
        cost_estimate=COST,
        compiler_params=pltpu.CompilerParams(vmem_limit_bytes=16 * 2**20),
    )(penalty, meta, own, *pulls, grad, grad_other, power, power_other)


def sums_kernel(first, planes, column, row, block, folded, arrived):
    count, length = column.shape
    depth, lots = arrived.shape
    size = length // lots

    def copies(k):
        return [
            pltpu.make_async_copy(
                planes.at[first + k, pl.ds(lot * size, size)],
                block.at[k % depth, pl.ds(lot * size, size)],
                arrived.at[k % depth, lot],
            )
            for lot in range(lots)
        ]

    for k in range(min(depth, count)):
        for copy in copies(k):
            copy.start()
    for k in range(count):
        for copy in copies(k):
            copy.wait()
        down, row[k : k + 1] = sum_plane(block.at[k % depth], folded, folded.shape[1])
        column[k : k + 1] = down.sum(0, keepdims=True)
        if k + depth < count:
            for copy in copies(k + depth):
                copy.start()


def volume_sums(planes, first, count, lanes):
    _, length, _ = planes.shape
    out = jax.ShapeDtypeStruct((count, length), jnp.float32)
    depth = min(count, 3)
    return pl.pallas_call(
        functools.partial(sums_kernel, first),
        out_shape=(out, out),
        in_specs=[HBM],
        out_specs=(VMEM, VMEM),
        scratch_shapes=[
            pltpu.VMEM((depth, length, length), jnp.float32),
            pltpu.VMEM((length, lanes), jnp.float32),
            pltpu.SemaphoreType.DMA((depth, 4)),
        ],
        cost_estimate=COST,
        compiler_params=pltpu.CompilerParams(vmem_limit_bytes=34 * 2**20),
    )(planes)


def pack_kernel(n_parts, penalty, *refs):
    parts, (lagrange, psi, packed) = refs[:n_parts], refs[n_parts:]
    owners, planes, _ = packed.shape
    owned = planes // 2
    for k in range(2):
        value = parts[0][k]
        for part in parts[1:]:
            value = value + part[k]
        psi[k] = value
        value = value + lagrange[k] / ratio_of(penalty)
        packed[:, k * owned : (k + 1) * owned, :] = value.reshape(owners, owned, value.shape[1])


def slice_kernel(views, angles, lines, *refs):
    sums, out = refs[:-1], refs[-1]
    column = jnp.concatenate([ref[...] for ref in sums[::2]], 0)
    row = jnp.concatenate([ref[...] for ref in sums[1::2]], 0)
    total, planes, width = lines.shape
    tiles = total // views
    length = column.shape[1]
    scale = 1.0 / math.sqrt(length)
    rows_of = lax.broadcasted_iota(jnp.int32, (width, width), 0)
    columns_of = lax.broadcasted_iota(jnp.int32, (width, width), 1)
    mirror = jnp.where(rows_of + columns_of == width - 1, 1.0, 0.0).astype(jnp.float32)

    def flip(values):
        stacked = jnp.dot(
            jnp.concatenate(values, 0),
            mirror,
            precision=HIGHEST,
            preferred_element_type=jnp.float32,
        )
        return [stacked[k * planes : (k + 1) * planes] for k in range(len(values))]

    base = []
    plain = []
    turned = []
    count = []
    for parity, source in ((0, column), (1, row)):
        for t in range(tiles):
            base.append(source[:, t * width : (t + 1) * width] * scale)
            plain.append(
                sum(
                    jnp.where(angles[u] == parity, lines[u * tiles + t], 0.0)
                    for u in range(views)
                )
            )
            turned.append(
                sum(
                    jnp.where(angles[u] == parity + 2, lines[u * tiles + tiles - 1 - t], 0.0)
                    for u in range(views)
                )
            )
        count.append(
            sum(
                jnp.where((angles[u] == parity) | (angles[u] == parity + 2), 1.0, 0.0)
                for u in range(views)
            )
        )
    turned = flip(turned)
    misfit = [
        base[parity * tiles + t] * count[parity]
        - plain[parity * tiles + t]
        - turned[parity * tiles + t]
        for parity in range(2)
        for t in range(tiles)
    ]
    total_of = [
        jnp.sum(
            functools.reduce(jnp.add, misfit[parity * tiles : (parity + 1) * tiles]),
            1,
            keepdims=True,
        )
        * (1.0 / length)
        for parity in range(2)
    ]
    fresh = [
        base[parity * tiles + t]
        - (misfit[parity * tiles + t] + total_of[1 - parity]) * (1.0 / views)
        for parity in range(2)
        for t in range(tiles)
    ]
    reversed_fresh = flip(fresh)
    for u in range(views):
        for t in range(tiles):
            out[u * tiles + t] = jnp.where(
                angles[u] == 0,
                fresh[t],
                jnp.where(
                    angles[u] == 1,
                    fresh[tiles + t],
                    jnp.where(
                        angles[u] == 2,
                        reversed_fresh[tiles - 1 - t],
                        reversed_fresh[2 * tiles - 1 - t],
                    ),
                ),
            )


def final_kernel(penalty, packed, psi, lagrange, fresh, renewed):
    owners, planes, width = packed.shape
    owned = planes // 2
    for k in range(2):
        value = packed[:, k * owned : (k + 1) * owned, :].reshape(owners * owned, width)
        fresh[k] = value
        renewed[k] = lagrange[k] + ratio_of(penalty) * (psi[k] - value)


def ratio_of(penalty):
    return penalty[0].astype(jnp.float32) / penalty[1].astype(jnp.float32)


def unpack_kernel(n_parts, *refs):
    parts, (probe, own, starts, held) = refs[:n_parts], refs[n_parts:]
    held[...] = probe[...]
    size = own.shape[1]
    for index, part in enumerate(parts):
        own[index] = part[:size]
        starts[index] = part[size:]


def shards(
    objects, probe, positions, amplitudes, reproj_prev, multipliers, volume, angles, penalty
):
    tiles = lax.axis_size("tile")
    views = lax.axis_size("view")
    routes = Routes(views, tiles)
    half = routes.half
    _, _, rows, tile_width = objects.shape
    width = probe.shape[2]
    total = tile_width * tiles
    chunks = total // width
    scans = positions.shape[1]
    owned = volume.shape[1]
    floor = 0.25 / math.sqrt(scans * tiles * width // total)
    lagrange = multipliers[0]
    measured = amplitudes[0]
    core = lax.rem(lax.axis_index("view"), 2)
    swapped = (lax.axis_index("tile") == routes.hubs[1]).astype(jnp.int32)
    dft_tables = tables(rows, width)

    def as_chunks(parts):
        joined = jnp.stack(parts, 0)
        if tile_width == width:
            return joined
        joined = joined.reshape(chunks // 2, width // tile_width, 2 * rows, tile_width)
        return joined.transpose(0, 2, 1, 3).reshape(chunks // 2, 2 * rows, width)

    def as_tiles(own):
        if tile_width == width:
            return [own[part].reshape(2, rows, width) for part in range(half)]
        parts = own.reshape(chunks // 2, 2 * rows, width // tile_width, tile_width)
        parts = parts.transpose(0, 2, 1, 3).reshape(half, 2, rows, tile_width)
        return [parts[part] for part in range(half)]

    direct = tile_width == width and half <= 4 and scans <= width
    pad = -scans % tile_width
    starts = jnp.pad(positions.astype(jnp.float32), ((0, 0), (0, pad)))
    starts = starts.reshape(-1, tile_width)
    starts = jnp.pad(starts, ((0, -starts.shape[0] % 8), (0, 0)))
    message = jnp.concatenate([objects.reshape(2 * rows, tile_width), starts], 0)
    arrived = [send(message, routes.to_hub(part, False)) for part in range(half)]
    ratio = jnp.broadcast_to(penalty.astype(jnp.float32)[:, None], (2, tile_width))
    ratio = lax.optimization_barrier(ratio)
    pull = (ratio[0] / ratio[1]) * reproj_prev[0] - lagrange
    near = [part for part in range(half) if part % 2 == 0]
    far = [part for part in range(half) if part % 2 == 1]
    planes = volume.reshape(2 * owned, total, total)
    levels = [None] * half
    if direct:
        pull, _ = lax.optimization_barrier((pull, message))
        measured = jnp.concatenate([measured, pull], 0)
        early, _ = lax.optimization_barrier((planes, measured))
        sums = [volume_sums(early, 0, owned, 128)]
        arrived, measured, sums[0] = lax.optimization_barrier((arrived, measured, sums[0]))
        for part in near:
            levels[part] = send(measured, routes.to_hub(part, True))
    else:
        sums = [volume_sums(planes, 0, owned, 128), volume_sums(planes, owned, owned, 128)]
        for part in range(half):
            levels[part] = send(measured, routes.to_hub(part, True))

    if direct:
        strips = jax.ShapeDtypeStruct((half, 2 * rows, width), jnp.float32)
        own, starts, probe = pl.pallas_call(
            functools.partial(unpack_kernel, half),
            out_shape=(
                strips,
                jax.ShapeDtypeStruct((half, 8, width), jnp.float32),
                jax.ShapeDtypeStruct(probe.shape, jnp.float32),
            ),
            in_specs=[VMEM] * (half + 1),
            out_specs=(VMEM, VMEM, VMEM),
            cost_estimate=COST,
        compiler_params=LIMIT,
        )(*arrived, probe)
        starts = starts[:, 0, :scans]
        pulls = levels
    else:
        levels = [jnp.stack(levels, 0)]
        own = as_chunks([part[: 2 * rows] for part in arrived])
        pull = pull.reshape(2 * rows, tile_width)
        pulls = [as_chunks([send(pull, routes.to_hub(part, False)) for part in range(half)])]
        starts = jnp.stack([part[2 * rows :].reshape(-1)[:scans] for part in arrived], 0)
    if direct:
        measured, own = lax.optimization_barrier((measured, own))
        relayed = send(measured, routes.relays())
        levels[far[1]] = send(measured, routes.to_hub(far[1], True))
        hop = jnp.where(core == 0, 0, tiles - 1) == lax.axis_index("tile")
        levels[far[0]] = send(jnp.where(hop, relayed, measured), routes.relayed(far[0]))
    other = send(own, routes.cores())
    meta = jnp.concatenate(
        [
            starts.reshape(-1).astype(jnp.int32),
            (core * (chunks // 2))[None],
            swapped[None],
        ]
    )
    power = illumination(meta, probe, chunks)
    power_other = send(power[chunks // 2 :], routes.cores())

    if direct:
        other, power, power_other = lax.optimization_barrier((other, power, power_other))
    calls = [near, far[1:], far[:1], near + far] if direct else [range(half)] * ITERS
    grad = None

    def run(parts, grad):
        measured = [levels[part] for part in parts] if direct else levels
        return gradient(
            meta, own, other, measured, parts, scans, probe, dft_tables, floor, grad
        )

    for parts in calls[:-1]:
        grad = run(parts, grad)
    for sweep in range(ITERS):
        grad_other = send(grad[chunks // 2 :], routes.cores())
        mine = update(penalty, meta, own, pulls, grad, grad_other, power, power_other)
        if sweep + 1 < ITERS:
            own = mine
            other = send(own, routes.cores())
            grad = run(calls[-1], None)

    parts = [send(part, routes.from_hub(index)) for index, part in enumerate(as_tiles(mine))]
    if direct:
        late, _ = lax.optimization_barrier((planes, mine))
        sums.append(volume_sums(late, owned, owned, 128))
        parts, sums[1] = lax.optimization_barrier((parts, sums[1]))
    strip = jax.ShapeDtypeStruct((2, rows, tile_width), jnp.float32)
    owners = views * tiles
    exchanged = jax.ShapeDtypeStruct((owners, 2 * owned, tile_width), jnp.float32)
    psi, packed = pl.pallas_call(
        functools.partial(pack_kernel, len(parts)),
        out_shape=(strip, exchanged),
        in_specs=[SMEM] + [VMEM] * (len(parts) + 1),
        out_specs=(VMEM, VMEM),
        cost_estimate=COST,
        compiler_params=LIMIT,
    )(penalty, *parts, lagrange)
    lines = lax.all_to_all(packed, AXES, split_axis=0, concat_axis=0, tiled=True)
    fresh = pl.pallas_call(
        functools.partial(slice_kernel, views),
        out_shape=exchanged,
        in_specs=[SMEM] + [VMEM] * 5,
        out_specs=VMEM,
        cost_estimate=COST,
        compiler_params=LIMIT,
    )(angles, lines, *sums[0], *sums[1])
    fresh = lax.all_to_all(fresh, AXES, split_axis=0, concat_axis=0, tiled=True)
    fresh_strip, renewed = pl.pallas_call(
        final_kernel,
        out_shape=(strip, strip),
        in_specs=[SMEM] + [VMEM] * 3,
        out_specs=(VMEM, VMEM),
        cost_estimate=COST,
        compiler_params=LIMIT,
    )(penalty, fresh, psi, lagrange)
    return (fresh_strip[None], renewed[None])


def solution(mesh):
    return jax.shard_map(
        shards,
        mesh=mesh,
        in_specs=(
            P("view", None, None, "tile"),
            P(),
            P("view", "tile"),
            P("view", "tile", None, None),
            P("view", None, None, "tile"),
            P("view", None, None, "tile"),
            P(None, ("view", "tile"), None, None),
            P(),
            P(),
        ),
        out_specs=(P("view", None, None, "tile"), P("view", None, None, "tile")),
        check_vma=False,
    )
```

```python
import functools
import math

import jax
import jax.numpy as jnp
import numpy as np
from jax import lax
from jax.experimental import pallas as pl
from jax.experimental.pallas import tpu as pltpu
from jax.sharding import PartitionSpec as P

ITERS = 2
AXES = ("view", "tile")
VMEM = pl.BlockSpec(memory_space=pltpu.VMEM)
SMEM = pl.BlockSpec(memory_space=pltpu.SMEM)
HBM = pl.BlockSpec(memory_space=pltpu.HBM)
COST = pl.CostEstimate(flops=0, bytes_accessed=0, transcendentals=0)
LIMIT = pltpu.CompilerParams(vmem_limit_bytes=16 * 2**20)
HIGHEST = lax.Precision.HIGHEST


class Routes:
    def __init__(self, views, tiles):
        self.views, self.tiles, self.half = views, tiles, tiles // 2
        self.hubs = (tiles // 4, tiles - 1 - tiles // 4)

    def at(self, view, tile):
        return view * self.tiles + tile

    def to_hub(self, part, swap):
        return [
            (
                self.at(2 * k + b, j * self.half + (self.turn(part, b) if swap else part)),
                self.at(2 * k + j, self.hubs[b]),
            )
            for k in range(self.views // 2)
            for b in range(2)
            for j in range(2)
        ]

    def from_hub(self, part):
        return [(target, source) for source, target in self.to_hub(part, False)]

    def turn(self, part, b):
        return self.half - 1 - part if b else part

    def relays(self):
        return [
            (self.at(v, tile), self.at(v, tile ^ 1))
            for v in range(self.views)
            for tile in ((self.tiles - 2 if v % 2 else 1),)
        ]

    def relayed(self, part):
        hops = dict(self.relays())
        return [(hops.get(source, source), target) for source, target in self.to_hub(part, True)]

    def cores(self):
        return [
            (self.at(v, t), self.at(v ^ 1, t)) for v in range(self.views) for t in range(self.tiles)
        ]


def send(value, pairs):
    return lax.ppermute(value, AXES, pairs)


def dft(length):
    indices = np.arange(length)
    phase = (indices[:, None] * indices[None, :] % length) * (2.0 * math.pi / length)
    return np.cos(phase) / math.sqrt(length), -np.sin(phase) / math.sqrt(length)


def halves(matrix):
    high = matrix.astype(jnp.bfloat16)
    return high, (matrix - high.astype(np.float64)).astype(jnp.bfloat16)


def tables(rows, width):
    result = []
    for length in (rows, width):
        cosine, sine = dft(length)
        for sign in (1.0, -1.0):
            result.append(halves(np.block([[cosine, -sign * sine], [sign * sine, cosine]])))
    return jnp.asarray(np.array(result[:2] if rows == width else result))


def split(value):
    high = value.astype(jnp.bfloat16)
    return high, (value - high.astype(jnp.float32)).astype(jnp.bfloat16)


def left(table, value):
    high, low = split(value)
    first, second = table
    return jnp.dot(
        jnp.concatenate([first, second, first], 1),
        jnp.concatenate([high, high, low], 0),
        preferred_element_type=jnp.float32,
    )


def right(value, table):
    high, low = split(value)
    first, second = table
    return jnp.dot(
        jnp.concatenate([high, high, low], 1),
        jnp.concatenate([first, second, first], 0),
        preferred_element_type=jnp.float32,
    )


def place(meta, index, chunks, width):
    start = meta[index]
    chunk = start // width
    offset = meta[meta.shape[0] - 2]
    here = lax.rem(chunk + offset, chunks)
    after = lax.rem(jnp.minimum(chunk + 1, chunks - 1) + offset, chunks)
    return here, after, start - chunk * width


def sum_plane(plane, folded, lanes):
    rows, length = plane.shape

    def step(index, down):
        base = pl.multiple_of(index * lanes, lanes)
        for at in range(0, lanes, 8):
            value = plane[pl.ds(base + at, 8)]
            down = down + value
            parts = [value[:, k : k + lanes] for k in range(0, length, lanes)]
            while len(parts) > 1:
                parts = [first + second for first, second in zip(parts[::2], parts[1::2])]
            folded[pl.ds(base + at, 8)] = parts[0]
        return down

    down = lax.fori_loop(0, rows // lanes, step, jnp.zeros((8, length), jnp.float32))
    lines = [folded[at : at + lanes].T.sum(0, keepdims=True) for at in range(0, rows, lanes)]
    return down, jnp.concatenate(lines, 1)


def gradient_kernel(floor, part_list, n_parts, first, scans, meta, own, other, *refs):
    measured, refs = refs[:n_parts], refs[n_parts:]
    probe, table, refs = refs[0], refs[1], refs[2:]
    if not first:
        before, refs = refs[0], refs[1:]
    grad, strip = refs
    chunks = strip.shape[0]
    _, rows, width = probe.shape
    strip[: chunks // 2] = own[:, : 2 * rows]
    strip[chunks // 2 :] = other[:, : 2 * rows]
    if first:
        grad[...] = jnp.zeros_like(grad)
    else:
        grad[...] = before[...]
    lane = lax.broadcasted_iota(jnp.int32, (rows, width), 1)
    probe_re = probe[0]
    probe_im = probe[1]
    swapped = meta[meta.shape[0] - 1]

    def get(index):
        return table[index, 0], table[index, 1]

    across = table.shape[0] - 2

    def work(part, amplitude, batch):
        row = part + swapped * (meta.shape[0] // scans - 1 - 2 * part)
        columns = []
        spots = []
        for j in range(batch):
            here, after, shift = place(meta, row * batch + j, chunks, width)
            spots.append((here, after, shift))
            back = lax.rem(width - shift, width)
            keep = lane < width - shift
            re, im = [
                jnp.where(
                    keep,
                    pltpu.roll(strip[here, k * rows : (k + 1) * rows], back, 1),
                    pltpu.roll(strip[after, k * rows : (k + 1) * rows], back, 1),
                )
                for k in range(2)
            ]
            columns.append(
                jnp.concatenate(
                    [probe_re * re - probe_im * im, probe_re * im + probe_im * re], 0
                )
            )
        mid = left(get(0), jnp.concatenate(columns, 1))
        mid = jnp.concatenate(
            [
                jnp.concatenate(
                    [
                        mid[:rows, j * width : (j + 1) * width],
                        mid[rows:, j * width : (j + 1) * width],
                    ],
                    1,
                )
                for j in range(batch)
            ],
            0,
        )
        far = right(mid, get(across + 1))
        far_re = far[:, :width]
        far_im = far[:, width:]
        level = amplitude[:batch].reshape(batch * rows, width)
        keep = 1.0 - level * jnp.minimum(
            lax.rsqrt(far_re * far_re + far_im * far_im), 1.0 / floor
        )
        mid = right(jnp.concatenate([far_re * keep, far_im * keep], 1), get(across))
        mid = jnp.concatenate(
            [
                jnp.concatenate(
                    [
                        mid[j * rows : (j + 1) * rows, :width],
                        mid[j * rows : (j + 1) * rows, width:],
                    ],
                    0,
                )
                for j in range(batch)
            ],
            1,
        )
        back = left(get(1), mid)
        for j in range(batch):
            here, after, shift = spots[j]
            back_re = back[:rows, j * width : (j + 1) * width]
            back_im = back[rows:, j * width : (j + 1) * width]
            inside = lane >= shift
            for k, value in enumerate(
                (
                    probe_re * back_re + probe_im * back_im,
                    probe_re * back_im - probe_im * back_re,
                )
            ):
                value = pltpu.roll(value, shift, 1)
                band = slice(k * rows, (k + 1) * rows)
                grad[here, band] += jnp.where(inside, value, 0.0)
                grad[after, band] += jnp.where(inside, 0.0, value)

    if len(part_list) == n_parts:
        for part, amplitude in zip(part_list, measured):
            work(part, amplitude, scans)
    else:

        def step(index, carry):
            work(index, measured[0].at[index], scans)
            return carry

        lax.fori_loop(0, measured[0].shape[0], step, 0)


def gradient(meta, own, other, measured, part_list, scans, probe, dft_tables, floor, before):
    _, rows, width = probe.shape
    chunks = own.shape[0] * 2
    shape = (chunks, 2 * rows, width)
    carried = [] if before is None else [before]
    count = 3 + len(measured) + 2
    return pl.pallas_call(
        functools.partial(
            gradient_kernel, floor, tuple(part_list), len(measured), before is None, scans
        ),
        out_shape=jax.ShapeDtypeStruct(shape, jnp.float32),
        in_specs=[SMEM] + [VMEM] * (count - 1 + len(carried)),
        out_specs=VMEM,
        scratch_shapes=[pltpu.VMEM(shape, jnp.float32)],
        input_output_aliases={} if before is None else {count: 0},
        cost_estimate=COST,
        compiler_params=pltpu.CompilerParams(vmem_limit_bytes=24 * 2**20),
    )(meta, own, other, *measured, probe, dft_tables, *carried)


def illumination_kernel(meta, probe, power):
    chunks = power.shape[0]
    _, rows, width = probe.shape
    power[...] = jnp.zeros_like(power)
    lane = lax.broadcasted_iota(jnp.int32, (rows, width), 1)
    value = probe[0] * probe[0] + probe[1] * probe[1]

    group = 8

    def step(index, carry):
        for j in range(group):
            here, after, shift = place(meta, index * group + j, chunks, width)
            rolled = pltpu.roll(value, shift, 1)
            power[here] += jnp.where(lane >= shift, rolled, 0.0)
            power[after] += jnp.where(lane >= shift, 0.0, rolled)
        return carry

    lax.fori_loop(0, (meta.shape[0] - 2) // group, step, 0)


def illumination(meta, probe, chunks):
    _, rows, width = probe.shape
    return pl.pallas_call(
        illumination_kernel,
        out_shape=jax.ShapeDtypeStruct((chunks, rows, width), jnp.float32),
        in_specs=[SMEM, VMEM],
        out_specs=VMEM,
        cost_estimate=COST,
        compiler_params=LIMIT,
    )(meta, probe)


def update_kernel(n_pull, penalty, meta, own, *refs):
    pulls, refs = refs[:n_pull], refs[n_pull:]
    grad, grad_other, power, power_other, out = refs
    count = out.shape[0]
    rows = power.shape[1]
    ratio = ratio_of(penalty)
    swapped = meta[meta.shape[0] - 1] == 1
    for chunk in range(count):
        inverse = 1.0 / (power[chunk] + power_other[chunk] + ratio)
        for k in range(2):
            band = slice(k * rows, (k + 1) * rows)
            old = own[chunk, band]
            if n_pull == 1:
                pull = pulls[0][chunk, band]
            else:
                last = pulls[0].shape[0] - 2 + k
                pull = jnp.where(swapped, pulls[count - 1 - chunk][last], pulls[chunk][last])
            step = grad[chunk, band] + grad_other[chunk, band] + ratio * old - pull
            out[chunk, band] = old - step * inverse


def update(penalty, meta, own, pulls, grad, grad_other, power, power_other):
    count = power_other.shape[0]
    return pl.pallas_call(
        functools.partial(update_kernel, len(pulls)),
        out_shape=jax.ShapeDtypeStruct((count,) + grad.shape[1:], jnp.float32),
        in_specs=[SMEM, SMEM] + [VMEM] * (len(pulls) + 5),
        out_specs=VMEM,
        cost_estimate=COST,
        compiler_params=pltpu.CompilerParams(vmem_limit_bytes=16 * 2**20),
    )(penalty, meta, own, *pulls, grad, grad_other, power, power_other)


def sums_kernel(first, planes, column, row, block, folded, arrived):
    count, length = column.shape
    depth, lots = arrived.shape
    size = length // lots

    def copies(k):
        return [
            pltpu.make_async_copy(
                planes.at[first + k, pl.ds(lot * size, size)],
                block.at[k % depth, pl.ds(lot * size, size)],
                arrived.at[k % depth, lot],
            )
            for lot in range(lots)
        ]

    for k in range(min(depth, count)):
        for copy in copies(k):
            copy.start()
    for k in range(count):
        for copy in copies(k):
            copy.wait()
        down, row[k : k + 1] = sum_plane(block.at[k % depth], folded, folded.shape[1])
        column[k : k + 1] = down.sum(0, keepdims=True)
        if k + depth < count:
            for copy in copies(k + depth):
                copy.start()


def volume_sums(planes, first, count, lanes):
    _, length, _ = planes.shape
    out = jax.ShapeDtypeStruct((count, length), jnp.float32)
    depth = min(count, 3)
    return pl.pallas_call(
        functools.partial(sums_kernel, first),
        out_shape=(out, out),
        in_specs=[HBM],
        out_specs=(VMEM, VMEM),
        scratch_shapes=[
            pltpu.VMEM((depth, length, length), jnp.float32),
            pltpu.VMEM((length, lanes), jnp.float32),
            pltpu.SemaphoreType.DMA((depth, 4)),
        ],
        cost_estimate=COST,
        compiler_params=pltpu.CompilerParams(vmem_limit_bytes=34 * 2**20),
    )(planes)


def pack_kernel(n_parts, penalty, *refs):
    parts, (lagrange, psi, packed) = refs[:n_parts], refs[n_parts:]
    owners, planes, _ = packed.shape
    owned = planes // 2
    for k in range(2):
        value = parts[0][k]
        for part in parts[1:]:
            value = value + part[k]
        psi[k] = value
        value = value + lagrange[k] / ratio_of(penalty)
        packed[:, k * owned : (k + 1) * owned, :] = value.reshape(owners, owned, value.shape[1])


def slice_kernel(views, angles, lines, *refs):
    sums, out = refs[:-1], refs[-1]
    column = jnp.concatenate([ref[...] for ref in sums[::2]], 0)
    row = jnp.concatenate([ref[...] for ref in sums[1::2]], 0)
    total, planes, width = lines.shape
    tiles = total // views
    length = column.shape[1]
    scale = 1.0 / math.sqrt(length)
    rows_of = lax.broadcasted_iota(jnp.int32, (width, width), 0)
    columns_of = lax.broadcasted_iota(jnp.int32, (width, width), 1)
    mirror = jnp.where(rows_of + columns_of == width - 1, 1.0, 0.0).astype(jnp.float32)

    def flip(values):
        stacked = jnp.dot(
            jnp.concatenate(values, 0),
            mirror,
            precision=HIGHEST,
            preferred_element_type=jnp.float32,
        )
        return [stacked[k * planes : (k + 1) * planes] for k in range(len(values))]

    base = []
    plain = []
    turned = []
    count = []
    for parity, source in ((0, column), (1, row)):
        for t in range(tiles):
            base.append(source[:, t * width : (t + 1) * width] * scale)
            plain.append(
                sum(
                    jnp.where(angles[u] == parity, lines[u * tiles + t], 0.0)
                    for u in range(views)
                )
            )
            turned.append(
                sum(
                    jnp.where(angles[u] == parity + 2, lines[u * tiles + tiles - 1 - t], 0.0)
                    for u in range(views)
                )
            )
        count.append(
            sum(
                jnp.where((angles[u] == parity) | (angles[u] == parity + 2), 1.0, 0.0)
                for u in range(views)
            )
        )
    turned = flip(turned)
    misfit = [
        base[parity * tiles + t] * count[parity]
        - plain[parity * tiles + t]
        - turned[parity * tiles + t]
        for parity in range(2)
        for t in range(tiles)
    ]
    total_of = [
        jnp.sum(
            functools.reduce(jnp.add, misfit[parity * tiles : (parity + 1) * tiles]),
            1,
            keepdims=True,
        )
        * (1.0 / length)
        for parity in range(2)
    ]
    fresh = [
        base[parity * tiles + t]
        - (misfit[parity * tiles + t] + total_of[1 - parity]) * (1.0 / views)
        for parity in range(2)
        for t in range(tiles)
    ]
    reversed_fresh = flip(fresh)
    for u in range(views):
        for t in range(tiles):
            out[u * tiles + t] = jnp.where(
                angles[u] == 0,
                fresh[t],
                jnp.where(
                    angles[u] == 1,
                    fresh[tiles + t],
                    jnp.where(
                        angles[u] == 2,
                        reversed_fresh[tiles - 1 - t],
                        reversed_fresh[2 * tiles - 1 - t],
                    ),
                ),
            )


def final_kernel(penalty, packed, psi, lagrange, fresh, renewed):
    owners, planes, width = packed.shape
    owned = planes // 2
    for k in range(2):
        value = packed[:, k * owned : (k + 1) * owned, :].reshape(owners * owned, width)
        fresh[k] = value
        renewed[k] = lagrange[k] + ratio_of(penalty) * (psi[k] - value)


def ratio_of(penalty):
    return penalty[0].astype(jnp.float32) / penalty[1].astype(jnp.float32)


def unpack_kernel(n_parts, *refs):
    parts, (probe, own, starts, held) = refs[:n_parts], refs[n_parts:]
    held[...] = probe[...]
    size = own.shape[1]
    for index, part in enumerate(parts):
        own[index] = part[:size]
        starts[index] = part[size:]


def shards(
    objects, probe, positions, amplitudes, reproj_prev, multipliers, volume, angles, penalty
):
    tiles = lax.axis_size("tile")
    views = lax.axis_size("view")
    routes = Routes(views, tiles)
    half = routes.half
    _, _, rows, tile_width = objects.shape
    width = probe.shape[2]
    total = tile_width * tiles
    chunks = total // width
    scans = positions.shape[1]
    owned = volume.shape[1]
    floor = 0.25 / math.sqrt(scans * tiles * width // total)
    lagrange = multipliers[0]
    measured = amplitudes[0]
    core = lax.rem(lax.axis_index("view"), 2)
    swapped = (lax.axis_index("tile") == routes.hubs[1]).astype(jnp.int32)
    dft_tables = tables(rows, width)

    def as_chunks(parts):
        joined = jnp.stack(parts, 0)
        if tile_width == width:
            return joined
        joined = joined.reshape(chunks // 2, width // tile_width, 2 * rows, tile_width)
        return joined.transpose(0, 2, 1, 3).reshape(chunks // 2, 2 * rows, width)

    def as_tiles(own):
        if tile_width == width:
            return [own[part].reshape(2, rows, width) for part in range(half)]
        parts = own.reshape(chunks // 2, 2 * rows, width // tile_width, tile_width)
        parts = parts.transpose(0, 2, 1, 3).reshape(half, 2, rows, tile_width)
        return [parts[part] for part in range(half)]

    direct = tile_width == width and half <= 4 and scans <= width
    pad = -scans % tile_width
    starts = jnp.pad(positions.astype(jnp.float32), ((0, 0), (0, pad)))
    starts = starts.reshape(-1, tile_width)
    starts = jnp.pad(starts, ((0, -starts.shape[0] % 8), (0, 0)))
    message = jnp.concatenate([objects.reshape(2 * rows, tile_width), starts], 0)
    arrived = [send(message, routes.to_hub(part, False)) for part in range(half)]
    ratio = jnp.broadcast_to(penalty.astype(jnp.float32)[:, None], (2, tile_width))
    ratio = lax.optimization_barrier(ratio)
    pull = (ratio[0] / ratio[1]) * reproj_prev[0] - lagrange
    near = [part for part in range(half) if part % 2 == 0]
    far = [part for part in range(half) if part % 2 == 1]
    planes = volume.reshape(2 * owned, total, total)
    levels = [None] * half
    cuts = (3 * owned // 4, 3 * owned // 2)
    if direct:
        pull, _ = lax.optimization_barrier((pull, message))
        measured = jnp.concatenate([measured, pull], 0)
        early, _ = lax.optimization_barrier((planes, measured))
        sums = [volume_sums(early, 0, cuts[0], 128)]
        arrived, measured, sums[0] = lax.optimization_barrier((arrived, measured, sums[0]))
        for part in near:
            levels[part] = send(measured, routes.to_hub(part, True))
    else:
        sums = [volume_sums(planes, 0, owned, 128), volume_sums(planes, owned, owned, 128)]
        for part in range(half):
            levels[part] = send(measured, routes.to_hub(part, True))

    if direct:
        strips = jax.ShapeDtypeStruct((half, 2 * rows, width), jnp.float32)
        own, starts, probe = pl.pallas_call(
            functools.partial(unpack_kernel, half),
            out_shape=(
                strips,
                jax.ShapeDtypeStruct((half, 8, width), jnp.float32),
                jax.ShapeDtypeStruct(probe.shape, jnp.float32),
            ),
            in_specs=[VMEM] * (half + 1),
            out_specs=(VMEM, VMEM, VMEM),
            cost_estimate=COST,
        compiler_params=LIMIT,
        )(*arrived, probe)
        starts = starts[:, 0, :scans]
        pulls = levels
    else:
        levels = [jnp.stack(levels, 0)]
        own = as_chunks([part[: 2 * rows] for part in arrived])
        pull = pull.reshape(2 * rows, tile_width)
        pulls = [as_chunks([send(pull, routes.to_hub(part, False)) for part in range(half)])]
        starts = jnp.stack([part[2 * rows :].reshape(-1)[:scans] for part in arrived], 0)
    if direct:
        measured, own = lax.optimization_barrier((measured, own))
        levels[far[1]] = send(measured, routes.to_hub(far[1], True))
    other = send(own, routes.cores())
    meta = jnp.concatenate(
        [
            starts.reshape(-1).astype(jnp.int32),
            (core * (chunks // 2))[None],
            swapped[None],
        ]
    )
    power = illumination(meta, probe, chunks)
    if direct:
        relayed = send(measured, routes.relays())
        hop = jnp.where(core == 0, 0, tiles - 1) == lax.axis_index("tile")
        levels[far[0]] = send(jnp.where(hop, relayed, measured), routes.relayed(far[0]))
    power_other = send(power[chunks // 2 :], routes.cores())

    if direct:
        middle, _ = lax.optimization_barrier((planes, own))
        sums.append(volume_sums(middle, cuts[0], cuts[1] - cuts[0], 128))
        other, power, power_other, sums[1] = lax.optimization_barrier(
            (other, power, power_other, sums[1])
        )
    calls = [near, far[1:] + far[:1], near + far] if direct else [range(half)] * ITERS
    grad = None

    def run(parts, grad):
        measured = [levels[part] for part in parts] if direct else levels
        return gradient(
            meta, own, other, measured, parts, scans, probe, dft_tables, floor, grad
        )

    for parts in calls[:-1]:
        grad = run(parts, grad)
    for sweep in range(ITERS):
        grad_other = send(grad[chunks // 2 :], routes.cores())
        mine = update(penalty, meta, own, pulls, grad, grad_other, power, power_other)
        if sweep + 1 < ITERS:
            own = mine
            other = send(own, routes.cores())
            grad = run(calls[-1], None)

    parts = [send(part, routes.from_hub(index)) for index, part in enumerate(as_tiles(mine))]
    if direct:
        late, _ = lax.optimization_barrier((planes, mine))
        sums.append(volume_sums(late, cuts[1], 2 * owned - cuts[1], 128))
        parts, sums[2] = lax.optimization_barrier((parts, sums[2]))
    strip = jax.ShapeDtypeStruct((2, rows, tile_width), jnp.float32)
    owners = views * tiles
    exchanged = jax.ShapeDtypeStruct((owners, 2 * owned, tile_width), jnp.float32)
    psi, packed = pl.pallas_call(
        functools.partial(pack_kernel, len(parts)),
        out_shape=(strip, exchanged),
        in_specs=[SMEM] + [VMEM] * (len(parts) + 1),
        out_specs=(VMEM, VMEM),
        cost_estimate=COST,
        compiler_params=LIMIT,
    )(penalty, *parts, lagrange)
    lines = lax.all_to_all(packed, AXES, split_axis=0, concat_axis=0, tiled=True)
    fresh = pl.pallas_call(
        functools.partial(slice_kernel, views),
        out_shape=exchanged,
        in_specs=[SMEM] + [VMEM] * (1 + 2 * len(sums)),
        out_specs=VMEM,
        cost_estimate=COST,
        compiler_params=LIMIT,
    )(angles, lines, *[line for pair in sums for line in pair])
    fresh = lax.all_to_all(fresh, AXES, split_axis=0, concat_axis=0, tiled=True)
    fresh_strip, renewed = pl.pallas_call(
        final_kernel,
        out_shape=(strip, strip),
        in_specs=[SMEM] + [VMEM] * 3,
        out_specs=(VMEM, VMEM),
        cost_estimate=COST,
        compiler_params=LIMIT,
    )(penalty, fresh, psi, lagrange)
    return (fresh_strip[None], renewed[None])


def solution(mesh):
    return jax.shard_map(
        shards,
        mesh=mesh,
        in_specs=(
            P("view", None, None, "tile"),
            P(),
            P("view", "tile"),
            P("view", "tile", None, None),
            P("view", None, None, "tile"),
            P("view", None, None, "tile"),
            P(None, ("view", "tile"), None, None),
            P(),
            P(),
        ),
        out_specs=(P("view", None, None, "tile"), P("view", None, None, "tile")),
        check_vma=False,
    )
```

```python
import functools
import math

import jax
import jax.numpy as jnp
import numpy as np
from jax import lax
from jax.experimental import pallas as pl
from jax.experimental.pallas import tpu as pltpu
from jax.sharding import PartitionSpec as P

ITERS = 2
AXES = ("view", "tile")
VMEM = pl.BlockSpec(memory_space=pltpu.VMEM)
SMEM = pl.BlockSpec(memory_space=pltpu.SMEM)
HBM = pl.BlockSpec(memory_space=pltpu.HBM)
COST = pl.CostEstimate(flops=0, bytes_accessed=0, transcendentals=0)
LIMIT = pltpu.CompilerParams(vmem_limit_bytes=16 * 2**20)
HIGHEST = lax.Precision.HIGHEST


class Routes:
    def __init__(self, views, tiles):
        self.views, self.tiles, self.half = views, tiles, tiles // 2
        self.hubs = (tiles // 4, tiles - 1 - tiles // 4)

    def at(self, view, tile):
        return view * self.tiles + tile

    def to_hub(self, part, swap):
        return [
            (
                self.at(2 * k + b, j * self.half + (self.turn(part, b) if swap else part)),
                self.at(2 * k + j, self.hubs[b]),
            )
            for k in range(self.views // 2)
            for b in range(2)
            for j in range(2)
        ]

    def from_hub(self, part):
        return [(target, source) for source, target in self.to_hub(part, False)]

    def turn(self, part, b):
        return self.half - 1 - part if b else part

    def relays(self):
        return [
            (self.at(v, tile), self.at(v, tile ^ 1))
            for v in range(self.views)
            for tile in ((self.tiles - 2 if v % 2 else 1),)
        ]

    def relayed(self, part):
        hops = dict(self.relays())
        return [(hops.get(source, source), target) for source, target in self.to_hub(part, True)]

    def cores(self):
        return [
            (self.at(v, t), self.at(v ^ 1, t)) for v in range(self.views) for t in range(self.tiles)
        ]


def send(value, pairs):
    return lax.ppermute(value, AXES, pairs)


def dft(length):
    indices = np.arange(length)
    phase = (indices[:, None] * indices[None, :] % length) * (2.0 * math.pi / length)
    return np.cos(phase) / math.sqrt(length), -np.sin(phase) / math.sqrt(length)


def halves(matrix):
    high = matrix.astype(jnp.bfloat16)
    return high, (matrix - high.astype(np.float64)).astype(jnp.bfloat16)


def tables(rows, width):
    result = []
    for length in (rows, width):
        cosine, sine = dft(length)
        for sign in (1.0, -1.0):
            result.append(halves(np.block([[cosine, -sign * sine], [sign * sine, cosine]])))
    return jnp.asarray(np.array(result[:2] if rows == width else result))


def split(value):
    high = value.astype(jnp.bfloat16)
    return high, (value - high.astype(jnp.float32)).astype(jnp.bfloat16)


def left(table, value):
    high, low = split(value)
    first, second = table
    return jnp.dot(
        jnp.concatenate([first, second, first], 1),
        jnp.concatenate([high, high, low], 0),
        preferred_element_type=jnp.float32,
    )


def right(value, table):
    high, low = split(value)
    first, second = table
    return jnp.dot(
        jnp.concatenate([high, high, low], 1),
        jnp.concatenate([first, second, first], 0),
        preferred_element_type=jnp.float32,
    )


def place(meta, index, chunks, width):
    start = meta[index]
    chunk = start // width
    offset = meta[meta.shape[0] - 2]
    here = lax.rem(chunk + offset, chunks)
    after = lax.rem(jnp.minimum(chunk + 1, chunks - 1) + offset, chunks)
    return here, after, start - chunk * width


def sum_plane(plane, folded, lanes):
    rows, length = plane.shape

    def step(index, down):
        base = pl.multiple_of(index * lanes, lanes)
        for at in range(0, lanes, 8):
            value = plane[pl.ds(base + at, 8)]
            down = down + value
            parts = [value[:, k : k + lanes] for k in range(0, length, lanes)]
            while len(parts) > 1:
                parts = [first + second for first, second in zip(parts[::2], parts[1::2])]
            folded[pl.ds(base + at, 8)] = parts[0]
        return down

    down = lax.fori_loop(0, rows // lanes, step, jnp.zeros((8, length), jnp.float32))
    lines = [folded[at : at + lanes].T.sum(0, keepdims=True) for at in range(0, rows, lanes)]
    return down, jnp.concatenate(lines, 1)


def gradient_kernel(floor, part_list, n_parts, first, scans, meta, own, other, *refs):
    measured, refs = refs[:n_parts], refs[n_parts:]
    probe, table, refs = refs[0], refs[1], refs[2:]
    if not first:
        before, refs = refs[0], refs[1:]
    grad, strip = refs
    chunks = strip.shape[0]
    _, rows, width = probe.shape
    strip[: chunks // 2] = own[:, : 2 * rows]
    strip[chunks // 2 :] = other[:, : 2 * rows]
    if first:
        grad[...] = jnp.zeros_like(grad)
    else:
        grad[...] = before[...]
    lane = lax.broadcasted_iota(jnp.int32, (rows, width), 1)
    probe_re = probe[0]
    probe_im = probe[1]
    swapped = meta[meta.shape[0] - 1]

    def get(index):
        return table[index, 0], table[index, 1]

    across = table.shape[0] - 2

    def work(part, amplitude, batch):
        row = part + swapped * (meta.shape[0] // scans - 1 - 2 * part)
        columns = []
        spots = []
        for j in range(batch):
            here, after, shift = place(meta, row * batch + j, chunks, width)
            spots.append((here, after, shift))
            back = lax.rem(width - shift, width)
            keep = lane < width - shift
            re, im = [
                jnp.where(
                    keep,
                    pltpu.roll(strip[here, k * rows : (k + 1) * rows], back, 1),
                    pltpu.roll(strip[after, k * rows : (k + 1) * rows], back, 1),
                )
                for k in range(2)
            ]
            columns.append(
                jnp.concatenate(
                    [probe_re * re - probe_im * im, probe_re * im + probe_im * re], 0
                )
            )
        mid = left(get(0), jnp.concatenate(columns, 1))
        mid = jnp.concatenate(
            [
                jnp.concatenate(
                    [
                        mid[:rows, j * width : (j + 1) * width],
                        mid[rows:, j * width : (j + 1) * width],
                    ],
                    1,
                )
                for j in range(batch)
            ],
            0,
        )
        far = right(mid, get(across + 1))
        far_re = far[:, :width]
        far_im = far[:, width:]
        level = amplitude[:batch].reshape(batch * rows, width)
        keep = 1.0 - level * jnp.minimum(
            lax.rsqrt(far_re * far_re + far_im * far_im), 1.0 / floor
        )
        mid = right(jnp.concatenate([far_re * keep, far_im * keep], 1), get(across))
        mid = jnp.concatenate(
            [
                jnp.concatenate(
                    [
                        mid[j * rows : (j + 1) * rows, :width],
                        mid[j * rows : (j + 1) * rows, width:],
                    ],
                    0,
                )
                for j in range(batch)
            ],
            1,
        )
        back = left(get(1), mid)
        for j in range(batch):
            here, after, shift = spots[j]
            back_re = back[:rows, j * width : (j + 1) * width]
            back_im = back[rows:, j * width : (j + 1) * width]
            inside = lane >= shift
            for k, value in enumerate(
                (
                    probe_re * back_re + probe_im * back_im,
                    probe_re * back_im - probe_im * back_re,
                )
            ):
                value = pltpu.roll(value, shift, 1)
                band = slice(k * rows, (k + 1) * rows)
                grad[here, band] += jnp.where(inside, value, 0.0)
                grad[after, band] += jnp.where(inside, 0.0, value)

    if len(part_list) == n_parts:
        for part, amplitude in zip(part_list, measured):
            work(part, amplitude, scans)
    else:

        def step(index, carry):
            work(index, measured[0].at[index], scans)
            return carry

        lax.fori_loop(0, measured[0].shape[0], step, 0)


def gradient(meta, own, other, measured, part_list, scans, probe, dft_tables, floor, before):
    _, rows, width = probe.shape
    chunks = own.shape[0] * 2
    shape = (chunks, 2 * rows, width)
    carried = [] if before is None else [before]
    count = 3 + len(measured) + 2
    return pl.pallas_call(
        functools.partial(
            gradient_kernel, floor, tuple(part_list), len(measured), before is None, scans
        ),
        out_shape=jax.ShapeDtypeStruct(shape, jnp.float32),
        in_specs=[SMEM] + [VMEM] * (count - 1 + len(carried)),
        out_specs=VMEM,
        scratch_shapes=[pltpu.VMEM(shape, jnp.float32)],
        input_output_aliases={} if before is None else {count: 0},
        cost_estimate=COST,
        compiler_params=pltpu.CompilerParams(vmem_limit_bytes=24 * 2**20),
    )(meta, own, other, *measured, probe, dft_tables, *carried)


def illumination_kernel(meta, probe, power):
    chunks = power.shape[0]
    _, rows, width = probe.shape
    power[...] = jnp.zeros_like(power)
    lane = lax.broadcasted_iota(jnp.int32, (rows, width), 1)
    value = probe[0] * probe[0] + probe[1] * probe[1]

    group = 8

    def step(index, carry):
        for j in range(group):
            here, after, shift = place(meta, index * group + j, chunks, width)
            rolled = pltpu.roll(value, shift, 1)
            power[here] += jnp.where(lane >= shift, rolled, 0.0)
            power[after] += jnp.where(lane >= shift, 0.0, rolled)
        return carry

    lax.fori_loop(0, (meta.shape[0] - 2) // group, step, 0)


def illumination(meta, probe, chunks):
    _, rows, width = probe.shape
    return pl.pallas_call(
        illumination_kernel,
        out_shape=jax.ShapeDtypeStruct((chunks, rows, width), jnp.float32),
        in_specs=[SMEM, VMEM],
        out_specs=VMEM,
        cost_estimate=COST,
        compiler_params=LIMIT,
    )(meta, probe)


def update_kernel(n_pull, penalty, meta, own, *refs):
    pulls, refs = refs[:n_pull], refs[n_pull:]
    grad, grad_other, power, power_other, out = refs
    count = out.shape[0]
    rows = power.shape[1]
    ratio = ratio_of(penalty)
    swapped = meta[meta.shape[0] - 1] == 1
    for chunk in range(count):
        inverse = 1.0 / (power[chunk] + power_other[chunk] + ratio)
        for k in range(2):
            band = slice(k * rows, (k + 1) * rows)
            old = own[chunk, band]
            if n_pull == 1:
                pull = pulls[0][chunk, band]
            else:
                last = pulls[0].shape[0] - 2 + k
                pull = jnp.where(swapped, pulls[count - 1 - chunk][last], pulls[chunk][last])
            step = grad[chunk, band] + grad_other[chunk, band] + ratio * old - pull
            out[chunk, band] = old - step * inverse


def update(penalty, meta, own, pulls, grad, grad_other, power, power_other):
    count = power_other.shape[0]
    return pl.pallas_call(
        functools.partial(update_kernel, len(pulls)),
        out_shape=jax.ShapeDtypeStruct((count,) + grad.shape[1:], jnp.float32),
        in_specs=[SMEM, SMEM] + [VMEM] * (len(pulls) + 5),
        out_specs=VMEM,
        cost_estimate=COST,
        compiler_params=pltpu.CompilerParams(vmem_limit_bytes=16 * 2**20),
    )(penalty, meta, own, *pulls, grad, grad_other, power, power_other)


def sums_kernel(first, planes, column, row, block, folded, arrived):
    count, length = column.shape
    depth, lots = arrived.shape
    size = length // lots

    def copies(k):
        return [
            pltpu.make_async_copy(
                planes.at[first + k, pl.ds(lot * size, size)],
                block.at[k % depth, pl.ds(lot * size, size)],
                arrived.at[k % depth, lot],
            )
            for lot in range(lots)
        ]

    for k in range(min(depth, count)):
        for copy in copies(k):
            copy.start()
    for k in range(count):
        for copy in copies(k):
            copy.wait()
        down, row[k : k + 1] = sum_plane(block.at[k % depth], folded, folded.shape[1])
        column[k : k + 1] = down.sum(0, keepdims=True)
        if k + depth < count:
            for copy in copies(k + depth):
                copy.start()


def volume_sums(planes, first, count, lanes):
    _, length, _ = planes.shape
    out = jax.ShapeDtypeStruct((count, length), jnp.float32)
    depth = min(count, 3)
    return pl.pallas_call(
        functools.partial(sums_kernel, first),
        out_shape=(out, out),
        in_specs=[HBM],
        out_specs=(VMEM, VMEM),
        scratch_shapes=[
            pltpu.VMEM((depth, length, length), jnp.float32),
            pltpu.VMEM((length, lanes), jnp.float32),
            pltpu.SemaphoreType.DMA((depth, 4)),
        ],
        cost_estimate=COST,
        compiler_params=pltpu.CompilerParams(vmem_limit_bytes=34 * 2**20),
    )(planes)


def pack_kernel(n_parts, penalty, *refs):
    parts, (lagrange, psi, packed) = refs[:n_parts], refs[n_parts:]
    owners, planes, _ = packed.shape
    owned = planes // 2
    for k in range(2):
        value = parts[0][k]
        for part in parts[1:]:
            value = value + part[k]
        psi[k] = value
        value = value + lagrange[k] / ratio_of(penalty)
        packed[:, k * owned : (k + 1) * owned, :] = value.reshape(owners, owned, value.shape[1])


def slice_kernel(views, angles, lines, *refs):
    sums, out = refs[:-1], refs[-1]
    column = jnp.concatenate([ref[...] for ref in sums[::2]], 0)
    row = jnp.concatenate([ref[...] for ref in sums[1::2]], 0)
    total, planes, width = lines.shape
    tiles = total // views
    length = column.shape[1]
    scale = 1.0 / math.sqrt(length)
    rows_of = lax.broadcasted_iota(jnp.int32, (width, width), 0)
    columns_of = lax.broadcasted_iota(jnp.int32, (width, width), 1)
    mirror = jnp.where(rows_of + columns_of == width - 1, 1.0, 0.0).astype(jnp.float32)

    def flip(values):
        stacked = jnp.dot(
            jnp.concatenate(values, 0),
            mirror,
            precision=HIGHEST,
            preferred_element_type=jnp.float32,
        )
        return [stacked[k * planes : (k + 1) * planes] for k in range(len(values))]

    base = []
    plain = []
    turned = []
    count = []
    for parity, source in ((0, column), (1, row)):
        for t in range(tiles):
            base.append(source[:, t * width : (t + 1) * width] * scale)
            plain.append(
                sum(
                    jnp.where(angles[u] == parity, lines[u * tiles + t], 0.0)
                    for u in range(views)
                )
            )
            turned.append(
                sum(
                    jnp.where(angles[u] == parity + 2, lines[u * tiles + tiles - 1 - t], 0.0)
                    for u in range(views)
                )
            )
        count.append(
            sum(
                jnp.where((angles[u] == parity) | (angles[u] == parity + 2), 1.0, 0.0)
                for u in range(views)
            )
        )
    turned = flip(turned)
    misfit = [
        base[parity * tiles + t] * count[parity]
        - plain[parity * tiles + t]
        - turned[parity * tiles + t]
        for parity in range(2)
        for t in range(tiles)
    ]
    total_of = [
        jnp.sum(
            functools.reduce(jnp.add, misfit[parity * tiles : (parity + 1) * tiles]),
            1,
            keepdims=True,
        )
        * (1.0 / length)
        for parity in range(2)
    ]
    fresh = [
        base[parity * tiles + t]
        - (misfit[parity * tiles + t] + total_of[1 - parity]) * (1.0 / views)
        for parity in range(2)
        for t in range(tiles)
    ]
    reversed_fresh = flip(fresh)
    for u in range(views):
        for t in range(tiles):
            out[u * tiles + t] = jnp.where(
                angles[u] == 0,
                fresh[t],
                jnp.where(
                    angles[u] == 1,
                    fresh[tiles + t],
                    jnp.where(
                        angles[u] == 2,
                        reversed_fresh[tiles - 1 - t],
                        reversed_fresh[2 * tiles - 1 - t],
                    ),
                ),
            )


def final_kernel(penalty, packed, psi, lagrange, fresh, renewed):
    owners, planes, width = packed.shape
    owned = planes // 2
    for k in range(2):
        value = packed[:, k * owned : (k + 1) * owned, :].reshape(owners * owned, width)
        fresh[k] = value
        renewed[k] = lagrange[k] + ratio_of(penalty) * (psi[k] - value)


def ratio_of(penalty):
    return penalty[0].astype(jnp.float32) / penalty[1].astype(jnp.float32)


def unpack_kernel(n_parts, *refs):
    parts, (probe, own, starts, held) = refs[:n_parts], refs[n_parts:]
    held[...] = probe[...]
    size = own.shape[1]
    for index, part in enumerate(parts):
        own[index] = part[:size]
        starts[index] = part[size:]


def shards(
    objects, probe, positions, amplitudes, reproj_prev, multipliers, volume, angles, penalty
):
    tiles = lax.axis_size("tile")
    views = lax.axis_size("view")
    routes = Routes(views, tiles)
    half = routes.half
    _, _, rows, tile_width = objects.shape
    width = probe.shape[2]
    total = tile_width * tiles
    chunks = total // width
    scans = positions.shape[1]
    owned = volume.shape[1]
    floor = 0.25 / math.sqrt(scans * tiles * width // total)
    lagrange = multipliers[0]
    measured = amplitudes[0]
    core = lax.rem(lax.axis_index("view"), 2)
    swapped = (lax.axis_index("tile") == routes.hubs[1]).astype(jnp.int32)
    dft_tables = tables(rows, width)

    def as_chunks(parts):
        joined = jnp.stack(parts, 0)
        if tile_width == width:
            return joined
        joined = joined.reshape(chunks // 2, width // tile_width, 2 * rows, tile_width)
        return joined.transpose(0, 2, 1, 3).reshape(chunks // 2, 2 * rows, width)

    def as_tiles(own):
        if tile_width == width:
            return [own[part].reshape(2, rows, width) for part in range(half)]
        parts = own.reshape(chunks // 2, 2 * rows, width // tile_width, tile_width)
        parts = parts.transpose(0, 2, 1, 3).reshape(half, 2, rows, tile_width)
        return [parts[part] for part in range(half)]

    direct = tile_width == width and half <= 4 and scans <= width and owned % 4 == 0
    pad = -scans % tile_width
    starts = jnp.pad(positions.astype(jnp.float32), ((0, 0), (0, pad)))
    starts = starts.reshape(-1, tile_width)
    starts = jnp.pad(starts, ((0, -starts.shape[0] % 8), (0, 0)))
    message = jnp.concatenate([objects.reshape(2 * rows, tile_width), starts], 0)
    arrived = [send(message, routes.to_hub(part, False)) for part in range(half)]
    ratio = jnp.broadcast_to(penalty.astype(jnp.float32)[:, None], (2, tile_width))
    ratio = lax.optimization_barrier(ratio)
    pull = (ratio[0] / ratio[1]) * reproj_prev[0] - lagrange
    near = [part for part in range(half) if part % 2 == 0]
    far = [part for part in range(half) if part % 2 == 1]
    planes = volume.reshape(2 * owned, total, total)
    levels = [None] * half
    cuts = (owned // 4, 7 * owned // 4)
    if direct:
        pull, _ = lax.optimization_barrier((pull, message))
        measured = jnp.concatenate([measured, pull], 0)
        for part in near:
            levels[part] = send(measured, routes.to_hub(part, True))
        early, _ = lax.optimization_barrier((planes, measured))
        sums = [volume_sums(early, 0, cuts[0], 128)]
        arrived, sums[0] = lax.optimization_barrier((arrived, sums[0]))
    else:
        sums = [volume_sums(planes, 0, owned, 128), volume_sums(planes, owned, owned, 128)]
        for part in range(half):
            levels[part] = send(measured, routes.to_hub(part, True))

    if direct:
        strips = jax.ShapeDtypeStruct((half, 2 * rows, width), jnp.float32)
        own, starts, probe = pl.pallas_call(
            functools.partial(unpack_kernel, half),
            out_shape=(
                strips,
                jax.ShapeDtypeStruct((half, 8, width), jnp.float32),
                jax.ShapeDtypeStruct(probe.shape, jnp.float32),
            ),
            in_specs=[VMEM] * (half + 1),
            out_specs=(VMEM, VMEM, VMEM),
            cost_estimate=COST,
        compiler_params=LIMIT,
        )(*arrived, probe)
        starts = starts[:, 0, :scans]
        pulls = levels
    else:
        levels = [jnp.stack(levels, 0)]
        own = as_chunks([part[: 2 * rows] for part in arrived])
        pull = pull.reshape(2 * rows, tile_width)
        pulls = [as_chunks([send(pull, routes.to_hub(part, False)) for part in range(half)])]
        starts = jnp.stack([part[2 * rows :].reshape(-1)[:scans] for part in arrived], 0)
    if direct:
        measured, own = lax.optimization_barrier((measured, own))
        levels[far[1]] = send(measured, routes.to_hub(far[1], True))
    other = send(own, routes.cores())
    meta = jnp.concatenate(
        [
            starts.reshape(-1).astype(jnp.int32),
            (core * (chunks // 2))[None],
            swapped[None],
        ]
    )
    power = illumination(meta, probe, chunks)
    if direct:
        relayed = send(measured, routes.relays())
        hop = jnp.where(core == 0, 0, tiles - 1) == lax.axis_index("tile")
        levels[far[0]] = send(jnp.where(hop, relayed, measured), routes.relayed(far[0]))
    power_other = send(power[chunks // 2 :], routes.cores())

    if direct:
        middle, _ = lax.optimization_barrier((planes, own))
        sums.append(volume_sums(middle, cuts[0], cuts[1] - cuts[0], 128))
        other, power, power_other, sums[1] = lax.optimization_barrier(
            (other, power, power_other, sums[1])
        )
    calls = [near, far[1:] + far[:1], near + far] if direct else [range(half)] * ITERS
    grad = None

    def run(parts, grad):
        measured = [levels[part] for part in parts] if direct else levels
        return gradient(
            meta, own, other, measured, parts, scans, probe, dft_tables, floor, grad
        )

    for parts in calls[:-1]:
        grad = run(parts, grad)
    for sweep in range(ITERS):
        grad_other = send(grad[chunks // 2 :], routes.cores())
        mine = update(penalty, meta, own, pulls, grad, grad_other, power, power_other)
        if sweep + 1 < ITERS:
            own = mine
            other = send(own, routes.cores())
            grad = run(calls[-1], None)

    parts = [send(part, routes.from_hub(index)) for index, part in enumerate(as_tiles(mine))]
    if direct:
        late, _ = lax.optimization_barrier((planes, mine))
        sums.append(volume_sums(late, cuts[1], 2 * owned - cuts[1], 128))
        parts, sums[2] = lax.optimization_barrier((parts, sums[2]))
    strip = jax.ShapeDtypeStruct((2, rows, tile_width), jnp.float32)
    owners = views * tiles
    exchanged = jax.ShapeDtypeStruct((owners, 2 * owned, tile_width), jnp.float32)
    psi, packed = pl.pallas_call(
        functools.partial(pack_kernel, len(parts)),
        out_shape=(strip, exchanged),
        in_specs=[SMEM] + [VMEM] * (len(parts) + 1),
        out_specs=(VMEM, VMEM),
        cost_estimate=COST,
        compiler_params=LIMIT,
    )(penalty, *parts, lagrange)
    lines = lax.all_to_all(packed, AXES, split_axis=0, concat_axis=0, tiled=True)
    fresh = pl.pallas_call(
        functools.partial(slice_kernel, views),
        out_shape=exchanged,
        in_specs=[SMEM] + [VMEM] * (1 + 2 * len(sums)),
        out_specs=VMEM,
        cost_estimate=COST,
        compiler_params=LIMIT,
    )(angles, lines, *[line for pair in sums for line in pair])
    fresh = lax.all_to_all(fresh, AXES, split_axis=0, concat_axis=0, tiled=True)
    fresh_strip, renewed = pl.pallas_call(
        final_kernel,
        out_shape=(strip, strip),
        in_specs=[SMEM] + [VMEM] * 3,
        out_specs=(VMEM, VMEM),
        cost_estimate=COST,
        compiler_params=LIMIT,
    )(penalty, fresh, psi, lagrange)
    return (fresh_strip[None], renewed[None])


def solution(mesh):
    return jax.shard_map(
        shards,
        mesh=mesh,
        in_specs=(
            P("view", None, None, "tile"),
            P(),
            P("view", "tile"),
            P("view", "tile", None, None),
            P("view", None, None, "tile"),
            P("view", None, None, "tile"),
            P(None, ("view", "tile"), None, None),
            P(),
            P(),
        ),
        out_specs=(P("view", None, None, "tile"), P("view", None, None, "tile")),
        check_vma=False,
    )
```

```python
import functools
import math

import jax
import jax.numpy as jnp
import numpy as np
from jax import lax
from jax.experimental import pallas as pl
from jax.experimental.pallas import tpu as pltpu
from jax.sharding import PartitionSpec as P

ITERS = 2
AXES = ("view", "tile")
VMEM = pl.BlockSpec(memory_space=pltpu.VMEM)
SMEM = pl.BlockSpec(memory_space=pltpu.SMEM)
HBM = pl.BlockSpec(memory_space=pltpu.HBM)
COST = pl.CostEstimate(flops=0, bytes_accessed=0, transcendentals=0)
LIMIT = pltpu.CompilerParams(vmem_limit_bytes=16 * 2**20)
HIGHEST = lax.Precision.HIGHEST


class Routes:
    def __init__(self, views, tiles):
        self.views, self.tiles, self.half = views, tiles, tiles // 2
        self.hubs = (tiles // 4, tiles - 1 - tiles // 4)

    def at(self, view, tile):
        return view * self.tiles + tile

    def to_hub(self, part, swap):
        return [
            (
                self.at(2 * k + b, j * self.half + (self.turn(part, b) if swap else part)),
                self.at(2 * k + j, self.hubs[b]),
            )
            for k in range(self.views // 2)
            for b in range(2)
            for j in range(2)
        ]

    def from_hub(self, part):
        return [(target, source) for source, target in self.to_hub(part, False)]

    def turn(self, part, b):
        return self.half - 1 - part if b else part

    def relays(self):
        return [
            (self.at(v, tile), self.at(v, tile ^ 1))
            for v in range(self.views)
            for tile in ((self.tiles - 2 if v % 2 else 1),)
        ]

    def relayed(self, part):
        hops = dict(self.relays())
        return [(hops.get(source, source), target) for source, target in self.to_hub(part, True)]

    def cores(self):
        return [
            (self.at(v, t), self.at(v ^ 1, t)) for v in range(self.views) for t in range(self.tiles)
        ]


def send(value, pairs):
    return lax.ppermute(value, AXES, pairs)


def dft(length):
    indices = np.arange(length)
    phase = (indices[:, None] * indices[None, :] % length) * (2.0 * math.pi / length)
    return np.cos(phase) / math.sqrt(length), -np.sin(phase) / math.sqrt(length)


def halves(matrix):
    high = matrix.astype(jnp.bfloat16)
    return high, (matrix - high.astype(np.float64)).astype(jnp.bfloat16)


def tables(rows, width):
    result = []
    for length in (rows, width):
        cosine, sine = dft(length)
        for sign in (1.0, -1.0):
            result.append(halves(np.block([[cosine, -sign * sine], [sign * sine, cosine]])))
    return jnp.asarray(np.array(result[:2] if rows == width else result))


def split(value):
    high = value.astype(jnp.bfloat16)
    return high, (value - high.astype(jnp.float32)).astype(jnp.bfloat16)


def left(table, value):
    high, low = split(value)
    first, second = table
    return jnp.dot(
        jnp.concatenate([first, second, first], 1),
        jnp.concatenate([high, high, low], 0),
        preferred_element_type=jnp.float32,
    )


def right(value, table):
    high, low = split(value)
    first, second = table
    return jnp.dot(
        jnp.concatenate([high, high, low], 1),
        jnp.concatenate([first, second, first], 0),
        preferred_element_type=jnp.float32,
    )


def place(meta, index, chunks, width):
    start = meta[index]
    chunk = start // width
    offset = meta[meta.shape[0] - 2]
    here = lax.rem(chunk + offset, chunks)
    after = lax.rem(jnp.minimum(chunk + 1, chunks - 1) + offset, chunks)
    return here, after, start - chunk * width


def sum_plane(plane, folded, lanes):
    rows, length = plane.shape

    def step(index, down):
        base = pl.multiple_of(index * lanes, lanes)
        for at in range(0, lanes, 8):
            value = plane[pl.ds(base + at, 8)]
            down = down + value
            parts = [value[:, k : k + lanes] for k in range(0, length, lanes)]
            while len(parts) > 1:
                parts = [first + second for first, second in zip(parts[::2], parts[1::2])]
            folded[pl.ds(base + at, 8)] = parts[0]
        return down

    down = lax.fori_loop(0, rows // lanes, step, jnp.zeros((8, length), jnp.float32))
    lines = [folded[at : at + lanes].T.sum(0, keepdims=True) for at in range(0, rows, lanes)]
    return down, jnp.concatenate(lines, 1)


def gradient_kernel(floor, part_list, n_parts, first, scans, meta, own, other, *refs):
    measured, refs = refs[:n_parts], refs[n_parts:]
    probe, table, refs = refs[0], refs[1], refs[2:]
    if not first:
        before, refs = refs[0], refs[1:]
    grad, strip = refs
    chunks = strip.shape[0]
    _, rows, width = probe.shape
    strip[: chunks // 2] = own[:, : 2 * rows]
    strip[chunks // 2 :] = other[:, : 2 * rows]
    if first:
        grad[...] = jnp.zeros_like(grad)
    else:
        grad[...] = before[...]
    lane = lax.broadcasted_iota(jnp.int32, (rows, width), 1)
    probe_re = probe[0]
    probe_im = probe[1]
    swapped = meta[meta.shape[0] - 1]

    def get(index):
        return table[index, 0], table[index, 1]

    across = table.shape[0] - 2

    def work(part, amplitude, batch):
        row = part + swapped * (meta.shape[0] // scans - 1 - 2 * part)
        columns = []
        spots = []
        for j in range(batch):
            here, after, shift = place(meta, row * batch + j, chunks, width)
            spots.append((here, after, shift))
            back = lax.rem(width - shift, width)
            keep = lane < width - shift
            re, im = [
                jnp.where(
                    keep,
                    pltpu.roll(strip[here, k * rows : (k + 1) * rows], back, 1),
                    pltpu.roll(strip[after, k * rows : (k + 1) * rows], back, 1),
                )
                for k in range(2)
            ]
            columns.append(
                jnp.concatenate(
                    [probe_re * re - probe_im * im, probe_re * im + probe_im * re], 0
                )
            )
        mid = left(get(0), jnp.concatenate(columns, 1))
        mid = jnp.concatenate(
            [
                jnp.concatenate(
                    [
                        mid[:rows, j * width : (j + 1) * width],
                        mid[rows:, j * width : (j + 1) * width],
                    ],
                    1,
                )
                for j in range(batch)
            ],
            0,
        )
        far = right(mid, get(across + 1))
        far_re = far[:, :width]
        far_im = far[:, width:]
        level = amplitude[:batch].reshape(batch * rows, width)
        keep = 1.0 - level * jnp.minimum(
            lax.rsqrt(far_re * far_re + far_im * far_im), 1.0 / floor
        )
        mid = right(jnp.concatenate([far_re * keep, far_im * keep], 1), get(across))
        mid = jnp.concatenate(
            [
                jnp.concatenate(
                    [
                        mid[j * rows : (j + 1) * rows, :width],
                        mid[j * rows : (j + 1) * rows, width:],
                    ],
                    0,
                )
                for j in range(batch)
            ],
            1,
        )
        back = left(get(1), mid)
        for j in range(batch):
            here, after, shift = spots[j]
            back_re = back[:rows, j * width : (j + 1) * width]
            back_im = back[rows:, j * width : (j + 1) * width]
            inside = lane >= shift
            for k, value in enumerate(
                (
                    probe_re * back_re + probe_im * back_im,
                    probe_re * back_im - probe_im * back_re,
                )
            ):
                value = pltpu.roll(value, shift, 1)
                band = slice(k * rows, (k + 1) * rows)
                grad[here, band] += jnp.where(inside, value, 0.0)
                grad[after, band] += jnp.where(inside, 0.0, value)

    if len(part_list) == n_parts:
        for part, amplitude in zip(part_list, measured):
            work(part, amplitude, scans)
    else:

        def step(index, carry):
            work(index, measured[0].at[index], scans)
            return carry

        lax.fori_loop(0, measured[0].shape[0], step, 0)


def gradient(meta, own, other, measured, part_list, scans, probe, dft_tables, floor, before):
    _, rows, width = probe.shape
    chunks = own.shape[0] * 2
    shape = (chunks, 2 * rows, width)
    carried = [] if before is None else [before]
    count = 3 + len(measured) + 2
    return pl.pallas_call(
        functools.partial(
            gradient_kernel, floor, tuple(part_list), len(measured), before is None, scans
        ),
        out_shape=jax.ShapeDtypeStruct(shape, jnp.float32),
        in_specs=[SMEM] + [VMEM] * (count - 1 + len(carried)),
        out_specs=VMEM,
        scratch_shapes=[pltpu.VMEM(shape, jnp.float32)],
        input_output_aliases={} if before is None else {count: 0},
        cost_estimate=COST,
        compiler_params=pltpu.CompilerParams(vmem_limit_bytes=24 * 2**20),
    )(meta, own, other, *measured, probe, dft_tables, *carried)


def illumination_kernel(meta, probe, power):
    chunks = power.shape[0]
    _, rows, width = probe.shape
    power[...] = jnp.zeros_like(power)
    lane = lax.broadcasted_iota(jnp.int32, (rows, width), 1)
    value = probe[0] * probe[0] + probe[1] * probe[1]

    group = 8

    def step(index, carry):
        for j in range(group):
            here, after, shift = place(meta, index * group + j, chunks, width)
            rolled = pltpu.roll(value, shift, 1)
            power[here] += jnp.where(lane >= shift, rolled, 0.0)
            power[after] += jnp.where(lane >= shift, 0.0, rolled)
        return carry

    lax.fori_loop(0, (meta.shape[0] - 2) // group, step, 0)


def illumination(meta, probe, chunks):
    _, rows, width = probe.shape
    return pl.pallas_call(
        illumination_kernel,
        out_shape=jax.ShapeDtypeStruct((chunks, rows, width), jnp.float32),
        in_specs=[SMEM, VMEM],
        out_specs=VMEM,
        cost_estimate=COST,
        compiler_params=LIMIT,
    )(meta, probe)


def update_kernel(n_pull, penalty, meta, own, *refs):
    pulls, refs = refs[:n_pull], refs[n_pull:]
    grad, grad_other, power, power_other, out = refs
    count = out.shape[0]
    rows = power.shape[1]
    ratio = ratio_of(penalty)
    swapped = meta[meta.shape[0] - 1] == 1
    for chunk in range(count):
        inverse = 1.0 / (power[chunk] + power_other[chunk] + ratio)
        for k in range(2):
            band = slice(k * rows, (k + 1) * rows)
            old = own[chunk, band]
            if n_pull == 1:
                pull = pulls[0][chunk, band]
            else:
                last = pulls[0].shape[0] - 2 + k
                pull = jnp.where(swapped, pulls[count - 1 - chunk][last], pulls[chunk][last])
            step = grad[chunk, band] + grad_other[chunk, band] + ratio * old - pull
            out[chunk, band] = old - step * inverse


def update(penalty, meta, own, pulls, grad, grad_other, power, power_other):
    count = power_other.shape[0]
    return pl.pallas_call(
        functools.partial(update_kernel, len(pulls)),
        out_shape=jax.ShapeDtypeStruct((count,) + grad.shape[1:], jnp.float32),
        in_specs=[SMEM, SMEM] + [VMEM] * (len(pulls) + 5),
        out_specs=VMEM,
        cost_estimate=COST,
        compiler_params=pltpu.CompilerParams(vmem_limit_bytes=16 * 2**20),
    )(penalty, meta, own, *pulls, grad, grad_other, power, power_other)


def sums_kernel(first, planes, column, row, block, folded, arrived):
    count, length = column.shape
    depth, lots = arrived.shape
    size = length // lots

    def copies(k):
        return [
            pltpu.make_async_copy(
                planes.at[first + k, pl.ds(lot * size, size)],
                block.at[k % depth, pl.ds(lot * size, size)],
                arrived.at[k % depth, lot],
            )
            for lot in range(lots)
        ]

    for k in range(min(depth, count)):
        for copy in copies(k):
            copy.start()
    for k in range(count):
        for copy in copies(k):
            copy.wait()
        down, row[k : k + 1] = sum_plane(block.at[k % depth], folded, folded.shape[1])
        column[k : k + 1] = down.sum(0, keepdims=True)
        if k + depth < count:
            for copy in copies(k + depth):
                copy.start()


def volume_sums(planes, first, count, lanes):
    _, length, _ = planes.shape
    out = jax.ShapeDtypeStruct((count, length), jnp.float32)
    depth = min(count, 3)
    return pl.pallas_call(
        functools.partial(sums_kernel, first),
        out_shape=(out, out),
        in_specs=[HBM],
        out_specs=(VMEM, VMEM),
        scratch_shapes=[
            pltpu.VMEM((depth, length, length), jnp.float32),
            pltpu.VMEM((length, lanes), jnp.float32),
            pltpu.SemaphoreType.DMA((depth, 4)),
        ],
        cost_estimate=COST,
        compiler_params=pltpu.CompilerParams(vmem_limit_bytes=34 * 2**20),
    )(planes)


def pack_kernel(n_parts, penalty, *refs):
    parts, (lagrange, psi, packed) = refs[:n_parts], refs[n_parts:]
    owners, planes, _ = packed.shape
    owned = planes // 2
    for k in range(2):
        value = parts[0][k]
        for part in parts[1:]:
            value = value + part[k]
        psi[k] = value
        value = value + lagrange[k] / ratio_of(penalty)
        packed[:, k * owned : (k + 1) * owned, :] = value.reshape(owners, owned, value.shape[1])


def slice_kernel(views, angles, lines, *refs):
    sums, out = refs[:-1], refs[-1]
    column = jnp.concatenate([ref[...] for ref in sums[::2]], 0)
    row = jnp.concatenate([ref[...] for ref in sums[1::2]], 0)
    total, planes, width = lines.shape
    tiles = total // views
    length = column.shape[1]
    scale = 1.0 / math.sqrt(length)
    rows_of = lax.broadcasted_iota(jnp.int32, (width, width), 0)
    columns_of = lax.broadcasted_iota(jnp.int32, (width, width), 1)
    mirror = jnp.where(rows_of + columns_of == width - 1, 1.0, 0.0).astype(jnp.float32)

    def flip(values):
        stacked = jnp.dot(
            jnp.concatenate(values, 0),
            mirror,
            precision=HIGHEST,
            preferred_element_type=jnp.float32,
        )
        return [stacked[k * planes : (k + 1) * planes] for k in range(len(values))]

    base = []
    plain = []
    turned = []
    count = []
    for parity, source in ((0, column), (1, row)):
        for t in range(tiles):
            base.append(source[:, t * width : (t + 1) * width] * scale)
            plain.append(
                sum(
                    jnp.where(angles[u] == parity, lines[u * tiles + t], 0.0)
                    for u in range(views)
                )
            )
            turned.append(
                sum(
                    jnp.where(angles[u] == parity + 2, lines[u * tiles + tiles - 1 - t], 0.0)
                    for u in range(views)
                )
            )
        count.append(
            sum(
                jnp.where((angles[u] == parity) | (angles[u] == parity + 2), 1.0, 0.0)
                for u in range(views)
            )
        )
    turned = flip(turned)
    misfit = [
        base[parity * tiles + t] * count[parity]
        - plain[parity * tiles + t]
        - turned[parity * tiles + t]
        for parity in range(2)
        for t in range(tiles)
    ]
    total_of = [
        jnp.sum(
            functools.reduce(jnp.add, misfit[parity * tiles : (parity + 1) * tiles]),
            1,
            keepdims=True,
        )
        * (1.0 / length)
        for parity in range(2)
    ]
    fresh = [
        base[parity * tiles + t]
        - (misfit[parity * tiles + t] + total_of[1 - parity]) * (1.0 / views)
        for parity in range(2)
        for t in range(tiles)
    ]
    reversed_fresh = flip(fresh)
    for u in range(views):
        for t in range(tiles):
            out[u * tiles + t] = jnp.where(
                angles[u] == 0,
                fresh[t],
                jnp.where(
                    angles[u] == 1,
                    fresh[tiles + t],
                    jnp.where(
                        angles[u] == 2,
                        reversed_fresh[tiles - 1 - t],
                        reversed_fresh[2 * tiles - 1 - t],
                    ),
                ),
            )


def final_kernel(penalty, packed, psi, lagrange, fresh, renewed):
    owners, planes, width = packed.shape
    owned = planes // 2
    for k in range(2):
        value = packed[:, k * owned : (k + 1) * owned, :].reshape(owners * owned, width)
        fresh[k] = value
        renewed[k] = lagrange[k] + ratio_of(penalty) * (psi[k] - value)


def ratio_of(penalty):
    return penalty[0].astype(jnp.float32) / penalty[1].astype(jnp.float32)


def unpack_kernel(n_parts, *refs):
    parts, (probe, own, starts, held) = refs[:n_parts], refs[n_parts:]
    held[...] = probe[...]
    size = own.shape[1]
    for index, part in enumerate(parts):
        own[index] = part[:size]
        starts[index] = part[size:]


def shards(
    objects, probe, positions, amplitudes, reproj_prev, multipliers, volume, angles, penalty
):
    tiles = lax.axis_size("tile")
    views = lax.axis_size("view")
    routes = Routes(views, tiles)
    half = routes.half
    _, _, rows, tile_width = objects.shape
    width = probe.shape[2]
    total = tile_width * tiles
    chunks = total // width
    scans = positions.shape[1]
    owned = volume.shape[1]
    floor = 0.25 / math.sqrt(scans * tiles * width // total)
    lagrange = multipliers[0]
    measured = amplitudes[0]
    core = lax.rem(lax.axis_index("view"), 2)
    swapped = (lax.axis_index("tile") == routes.hubs[1]).astype(jnp.int32)
    dft_tables = tables(rows, width)

    def as_chunks(parts):
        joined = jnp.stack(parts, 0)
        if tile_width == width:
            return joined
        joined = joined.reshape(chunks // 2, width // tile_width, 2 * rows, tile_width)
        return joined.transpose(0, 2, 1, 3).reshape(chunks // 2, 2 * rows, width)

    def as_tiles(own):
        if tile_width == width:
            return [own[part].reshape(2, rows, width) for part in range(half)]
        parts = own.reshape(chunks // 2, 2 * rows, width // tile_width, tile_width)
        parts = parts.transpose(0, 2, 1, 3).reshape(half, 2, rows, tile_width)
        return [parts[part] for part in range(half)]

    direct = tile_width == width and half <= 4 and scans <= width and owned % 4 == 0
    pad = -scans % tile_width
    starts = jnp.pad(positions.astype(jnp.float32), ((0, 0), (0, pad)))
    starts = starts.reshape(-1, tile_width)
    starts = jnp.pad(starts, ((0, -starts.shape[0] % 8), (0, 0)))
    message = jnp.concatenate([objects.reshape(2 * rows, tile_width), starts], 0)
    arrived = [send(message, routes.to_hub(part, False)) for part in range(half)]
    ratio = jnp.broadcast_to(penalty.astype(jnp.float32)[:, None], (2, tile_width))
    ratio = lax.optimization_barrier(ratio)
    pull = (ratio[0] / ratio[1]) * reproj_prev[0] - lagrange
    near = [part for part in range(half) if part % 2 == 0]
    far = [part for part in range(half) if part % 2 == 1]
    planes = volume.reshape(2 * owned, total, total)
    levels = [None] * half
    cuts = (owned // 4, 3 * owned // 2)
    if direct:
        pull, _ = lax.optimization_barrier((pull, message))
        measured = jnp.concatenate([measured, pull], 0)
        for part in near:
            levels[part] = send(measured, routes.to_hub(part, True))
        early, _ = lax.optimization_barrier((planes, measured))
        sums = [volume_sums(early, 0, cuts[0], 128)]
        arrived, sums[0] = lax.optimization_barrier((arrived, sums[0]))
    else:
        sums = [volume_sums(planes, 0, owned, 128), volume_sums(planes, owned, owned, 128)]
        for part in range(half):
            levels[part] = send(measured, routes.to_hub(part, True))

    if direct:
        strips = jax.ShapeDtypeStruct((half, 2 * rows, width), jnp.float32)
        own, starts, probe = pl.pallas_call(
            functools.partial(unpack_kernel, half),
            out_shape=(
                strips,
                jax.ShapeDtypeStruct((half, 8, width), jnp.float32),
                jax.ShapeDtypeStruct(probe.shape, jnp.float32),
            ),
            in_specs=[VMEM] * (half + 1),
            out_specs=(VMEM, VMEM, VMEM),
            cost_estimate=COST,
        compiler_params=LIMIT,
        )(*arrived, probe)
        starts = starts[:, 0, :scans]
        pulls = levels
    else:
        levels = [jnp.stack(levels, 0)]
        own = as_chunks([part[: 2 * rows] for part in arrived])
        pull = pull.reshape(2 * rows, tile_width)
        pulls = [as_chunks([send(pull, routes.to_hub(part, False)) for part in range(half)])]
        starts = jnp.stack([part[2 * rows :].reshape(-1)[:scans] for part in arrived], 0)
    if direct:
        measured, own = lax.optimization_barrier((measured, own))
        levels[far[1]] = send(measured, routes.to_hub(far[1], True))
    other = send(own, routes.cores())
    meta = jnp.concatenate(
        [
            starts.reshape(-1).astype(jnp.int32),
            (core * (chunks // 2))[None],
            swapped[None],
        ]
    )
    power = illumination(meta, probe, chunks)
    if direct:
        relayed = send(measured, routes.relays())
        hop = jnp.where(core == 0, 0, tiles - 1) == lax.axis_index("tile")
        levels[far[0]] = send(jnp.where(hop, relayed, measured), routes.relayed(far[0]))
    power_other = send(power[chunks // 2 :], routes.cores())

    if direct:
        middle, _ = lax.optimization_barrier((planes, own))
        sums.append(volume_sums(middle, cuts[0], cuts[1] - cuts[0], 128))
        other, power, power_other, sums[1] = lax.optimization_barrier(
            (other, power, power_other, sums[1])
        )
    calls = [near, far[1:] + far[:1], near + far] if direct else [range(half)] * ITERS
    grad = None

    def run(parts, grad):
        measured = [levels[part] for part in parts] if direct else levels
        return gradient(
            meta, own, other, measured, parts, scans, probe, dft_tables, floor, grad
        )

    for parts in calls[:-1]:
        grad = run(parts, grad)
    for sweep in range(ITERS):
        grad_other = send(grad[chunks // 2 :], routes.cores())
        mine = update(penalty, meta, own, pulls, grad, grad_other, power, power_other)
        if sweep + 1 < ITERS:
            own = mine
            other = send(own, routes.cores())
            grad = run(calls[-1], None)

    parts = [send(part, routes.from_hub(index)) for index, part in enumerate(as_tiles(mine))]
    if direct:
        late, _ = lax.optimization_barrier((planes, mine))
        sums.append(volume_sums(late, cuts[1], 2 * owned - cuts[1], 128))
        parts, sums[2] = lax.optimization_barrier((parts, sums[2]))
    strip = jax.ShapeDtypeStruct((2, rows, tile_width), jnp.float32)
    owners = views * tiles
    exchanged = jax.ShapeDtypeStruct((owners, 2 * owned, tile_width), jnp.float32)
    psi, packed = pl.pallas_call(
        functools.partial(pack_kernel, len(parts)),
        out_shape=(strip, exchanged),
        in_specs=[SMEM] + [VMEM] * (len(parts) + 1),
        out_specs=(VMEM, VMEM),
        cost_estimate=COST,
        compiler_params=LIMIT,
    )(penalty, *parts, lagrange)
    lines = lax.all_to_all(packed, AXES, split_axis=0, concat_axis=0, tiled=True)
    fresh = pl.pallas_call(
        functools.partial(slice_kernel, views),
        out_shape=exchanged,
        in_specs=[SMEM] + [VMEM] * (1 + 2 * len(sums)),
        out_specs=VMEM,
        cost_estimate=COST,
        compiler_params=LIMIT,
    )(angles, lines, *[line for pair in sums for line in pair])
    fresh = lax.all_to_all(fresh, AXES, split_axis=0, concat_axis=0, tiled=True)
    fresh_strip, renewed = pl.pallas_call(
        final_kernel,
        out_shape=(strip, strip),
        in_specs=[SMEM] + [VMEM] * 3,
        out_specs=(VMEM, VMEM),
        cost_estimate=COST,
        compiler_params=LIMIT,
    )(penalty, fresh, psi, lagrange)
    return (fresh_strip[None], renewed[None])


def solution(mesh):
    return jax.shard_map(
        shards,
        mesh=mesh,
        in_specs=(
            P("view", None, None, "tile"),
            P(),
            P("view", "tile"),
            P("view", "tile", None, None),
            P("view", None, None, "tile"),
            P("view", None, None, "tile"),
            P(None, ("view", "tile"), None, None),
            P(),
            P(),
        ),
        out_specs=(P("view", None, None, "tile"), P("view", None, None, "tile")),
        check_vma=False,
    )
```
